128 devices in a mesh: dp: 16 (over z, y), seq: 8 (over x, core).
Axes of the slice: x: 4, y: 4, z: 4, core: 2. Of those that a mesh axis runs over, the one named last changes fastest.
Arguments:
- acts: bfloat16 [32, 512, 4608], P('dp', 'seq'), may hold values from -20 to 20, as said below
- grads: bfloat16 [32, 512, 18432], P('dp', 'seq'), may hold values from -0.00045670236 to 0.00045670236, as said below
Outputs:
- update: bfloat16 [4608, 18432], P('dp', 'seq')
- norms: float32 [32], P('dp')
The draws below stay inside these ranges and needn't reach their ends.
Inputs may be any that keep to these rules, and one draw needn't show every extreme that they name: `acts`: entries of order one. `grads`: independent entries, small: magnitudes under 2000 / (21 * sqrt(43486543872)).
All inputs are finite; a program needn't handle non-finite values.
Results may differ from the reference program's by a relative error of at most 0.025.
Values may be sent and summed in bfloat16 or wider, within the bound.
No kernel may reach another device: no remote copies, remote signals or barrier semaphores. Data moves between devices by JAX's collectives and lax.ppermute only.
A program may use at most 128 MiB of HBM per device.

```python
import math
import jax
import jax.numpy as jnp
from jax import lax

D = 4608
FF = 18432
LEN = 512
SEQ_DEV = 2
SEQS = 32
N_DP = 16


def draw_acts(key, part):
    key = jax.random.fold_in(key, 11)
    knoise, krow, kcol = jax.random.split(key, 3)
    row_clip_scale = jnp.exp(jax.random.uniform(krow, (SEQS, LEN, 1), jnp.float32) * math.log(10.0))
    col_scale = jnp.exp(jax.random.uniform(kcol, (1, 1, D), jnp.float32) * math.log(10.0))
    base = jnp.clip(jax.random.normal(knoise, (SEQS, LEN, D), jnp.float32), -4.0, 4.0)
    return (base * row_clip_scale * col_scale / 21.0).astype(jnp.bfloat16)


def rising(count, slope):
    position = jnp.arange(count, dtype=jnp.float32) / (count - 1)
    return (1.0 + slope * position) / (1.0 + slope)


def draw_grads(key, part):
    key = jax.random.fold_in(key, 23)
    knoise, krow, kcol, kexample = jax.random.split(key, 4)
    row_clip_scale = jnp.exp(jax.random.uniform(krow, (SEQS, LEN, 1), jnp.float32) * math.log(10.0))
    col_scale = jnp.exp(jax.random.uniform(kcol, (1, 1, FF), jnp.float32) * math.log(10.0))
    example_scale = jnp.exp(jax.random.uniform(kexample, (SEQS, 1, 1), jnp.float32, math.log(0.3), math.log(3.0)))
    token_ramp = rising(LEN, 2.0).reshape(1, LEN, 1)
    column_ramp = rising(FF, 2.0).reshape(1, 1, FF)
    base = jnp.clip(jax.random.normal(knoise, (SEQS, LEN, FF), jnp.float32), -4.0, 4.0)
    scale = example_scale * token_ramp * column_ramp * 1.44 / (21.0 * math.sqrt(LEN * D * FF))
    return (base * row_clip_scale * col_scale * scale).astype(jnp.bfloat16)


def setup_inputs(seed: int = 0) -> dict:
    keys = jax.random.split(jax.random.key(seed), 3)
    acts = draw_acts(jax.random.fold_in(keys[2], 71), 0)
    grads = draw_grads(jax.random.fold_in(keys[2], 71), 0)
    return dict(acts=acts, grads=grads)


def per_example_norm(pair):
    x, g = pair
    xf = x.astype(jnp.float32)
    gf = g.astype(jnp.float32)
    activation_gram_matrix = jnp.dot(xf, xf.T, preferred_element_type=jnp.float32)
    gradient_gram_matrix = jnp.dot(gf, gf.T, preferred_element_type=jnp.float32)
    return jnp.sqrt(jnp.sum(activation_gram_matrix * gradient_gram_matrix))

def reference(acts, grads):
    norms = lax.map(per_example_norm, (acts, grads))
    clip = jnp.minimum(1.0, 1.0 / (norms + 1e-06))
    factor = math.sqrt(D * FF / SEQS)
    scaled = (grads * (clip * factor)[:, None, None]).astype(jnp.bfloat16)
    group_x = acts.reshape(N_DP, SEQ_DEV * LEN, D)
    group_z = scaled.reshape(N_DP, SEQ_DEV * LEN, FF)

    def add_group(total, pair):
        x, z = pair
        term = jnp.dot(x.astype(jnp.float32).T, z.astype(jnp.float32), preferred_element_type=jnp.float32)
        return (total + term.astype(jnp.bfloat16).astype(jnp.float32), None)
    total, _ = lax.scan(add_group, jnp.zeros((D, FF), jnp.float32), (group_x, group_z))
    return (total.astype(jnp.bfloat16), norms)
```

```python
import functools
import math

import jax
import jax.numpy as jnp
from jax import lax
from jax.experimental import pallas as pl
from jax.experimental.pallas import tpu as pltpu
from jax.sharding import PartitionSpec as P

ORDERS = ((4, 12, 1, 3), (12, 4, 3, 1), (1, 3, 4, 12), (3, 1, 12, 4))
WIDTHS = (640, 640, 512, 512)


def block_order(masks):
    order = [0]
    for mask in reversed(masks):
        order = order + [mask ^ k for k in order]
    return order


def exchange(value, axis, mask):
    return lax.ppermute(value, axis, [(i, i ^ mask) for i in range(lax.axis_size(axis))])


def product_kernel(index_ref, *refs):
    *a_refs, g_ref, out_ref = refs
    rows = jnp.concatenate([a[0] for a in a_refs], axis=0)
    out_ref[...] = jnp.dot(rows, g_ref[...], preferred_element_type=jnp.float32).astype(out_ref.dtype)


def product(a_blocks, g, index, group):
    count = index.shape[0]
    _, block, tokens = a_blocks.shape
    width = g.shape[1]
    a_specs = [
        pl.BlockSpec((1, block, tokens), functools.partial(lambda j, i, index_ref: (index_ref[i * group + j], 0, 0), j))
        for j in range(group)
    ]
    return pl.pallas_call(
        product_kernel,
        grid_spec=pltpu.PrefetchScalarGridSpec(
            num_scalar_prefetch=1,
            grid=(count // group,),
            in_specs=[*a_specs, pl.BlockSpec((tokens, width), lambda i, index_ref: (0, 0))],
            out_specs=pl.BlockSpec((group * block, width), lambda i, index_ref: (i, 0)),
        ),
        out_shape=jax.ShapeDtypeStruct((count * block, width), jnp.bfloat16),
        compiler_params=pltpu.CompilerParams(vmem_limit_bytes=40 * 1024 * 1024),
        cost_estimate=pl.CostEstimate(
            flops=2 * count * block * tokens * width,
            bytes_accessed=2 * (count * block * tokens + tokens * width + count * block * width),
            transcendentals=0,
        ),
    )(index, *([a_blocks] * group), g)


def turn_kernel(in_ref, out_ref):
    out_ref[...] = in_ref[...].T


def turn(value):
    tokens, width = value.shape
    step = 4
    return pl.pallas_call(
        turn_kernel,
        grid=(step,),
        in_specs=[pl.BlockSpec((tokens, width // step), lambda i: (0, i))],
        out_specs=pl.BlockSpec((width // step, tokens), lambda i: (i, 0)),
        out_shape=jax.ShapeDtypeStruct((width, tokens), value.dtype),
    )(value)


def join_kernel(in_ref, out_ref):
    for s in range(in_ref.shape[0]):
        out_ref[:, s * in_ref.shape[2] : (s + 1) * in_ref.shape[2]] = in_ref[s]


def join(value):
    n, rows, lanes = value.shape
    step = 8
    return pl.pallas_call(
        join_kernel,
        grid=(step,),
        in_specs=[pl.BlockSpec((n, rows // step, lanes), lambda i: (0, i, 0))],
        out_specs=pl.BlockSpec((rows // step, n * lanes), lambda i: (i, 0)),
        out_shape=jax.ShapeDtypeStruct((rows, n * lanes), value.dtype),
    )(value)


def split_kernel(in_ref, *out_refs):
    low = 0
    for out_ref in out_refs:
        size = out_ref.shape[2]
        out_ref[0] = in_ref[:, low : low + size]
        low += size


def split(value, n, widths):
    rows, total = value.shape
    return pl.pallas_call(
        split_kernel,
        grid=(n,),
        in_specs=[pl.BlockSpec((rows, total // n), lambda i: (0, i))],
        out_specs=[pl.BlockSpec((1, rows, w), lambda i: (i, 0, 0)) for w in widths],
        out_shape=[jax.ShapeDtypeStruct((n, rows, w), value.dtype) for w in widths],
    )(value)


def add(a, b):
    return (a.astype(jnp.float32) + b.astype(jnp.float32)).astype(jnp.bfloat16)


def on_device(acts, grads):
    seq_count = lax.axis_size("seq")
    replica_count = lax.axis_size("dp")
    examples, local_len, width = acts.shape
    hidden = grads.shape[2]
    local = examples * local_len
    tokens = seq_count * local
    block = width // replica_count
    me = lax.axis_index("dp")

    a_t = join(lax.all_gather(turn(acts.reshape(local, width)), "seq", axis=0))
    example = (jnp.arange(tokens) // local_len) % examples
    same = example[:, None] == example[None, :]
    act_gram = lax.dot_general(a_t, a_t, (((0,), (0,)), ((), ())), preferred_element_type=jnp.float32)
    act_gram = jnp.where(same, act_gram, 0.0)

    parts = []
    rows_sum = jnp.zeros((tokens,), jnp.float32)
    for piece in split(grads.reshape(local, hidden), seq_count, WIDTHS):
        piece = lax.all_to_all(piece, "seq", split_axis=0, concat_axis=0, tiled=True)
        piece = piece.reshape(tokens, -1)
        gram = lax.dot_general(piece, piece, (((1,), (1,)), ((), ())), preferred_element_type=jnp.float32)
        rows_sum = rows_sum + jnp.sum(act_gram * gram, axis=1)
        parts.append(piece)
    partial_value = jnp.sum(rows_sum.reshape(seq_count, examples, local_len), axis=(0, 2))
    norms = jnp.sqrt(lax.psum(partial_value, "seq"))
    clip = jnp.minimum(1.0, 1.0 / (norms + 1e-06))
    factor = math.sqrt(width * hidden / (examples * replica_count))
    scale = jnp.tile(jnp.repeat(clip * factor, local_len), seq_count)[:, None]

    a_blocks = a_t.reshape(replica_count, block, tokens)
    outs = []
    for masks, piece in zip(ORDERS, parts):
        scaled = (piece * scale).astype(jnp.bfloat16)
        order = me ^ jnp.array(block_order(masks), jnp.int32)
        half = replica_count // 2
        send = product(a_blocks, scaled, order[half:], 4)
        keep = product(a_blocks, scaled, order[:half], 4)
        received = exchange(send, "dp", masks[0])
        for mask in masks[1:]:
            rows = keep.shape[0] // 2
            send = add(keep[rows:], received[rows:])
            sent = exchange(send, "dp", mask)
            keep = add(keep[:rows], received[:rows])
            received = sent
        outs.append(add(keep, received))
    return (jnp.concatenate(outs, axis=1), norms)


def solution(mesh):
    return jax.shard_map(
        on_device,
        mesh=mesh,
        in_specs=(P("dp", "seq", None), P("dp", "seq", None)),
        out_specs=(P("dp", "seq"), P("dp")),
        check_vma=False,
    )
```

```python
import functools
import math

import jax
import jax.numpy as jnp
from jax import lax
from jax.experimental import pallas as pl
from jax.experimental.pallas import tpu as pltpu
from jax.sharding import PartitionSpec as P

ORDERS = ((4, 12, 1, 3), (12, 4, 3, 1), (1, 3, 4, 12), (3, 1, 12, 4))
WIDTHS = (640, 640, 512, 512)


def block_order(masks):
    order = [0]
    for mask in reversed(masks):
        order = order + [mask ^ k for k in order]
    return order


def exchange(value, axis, mask):
    return lax.ppermute(value, axis, [(i, i ^ mask) for i in range(lax.axis_size(axis))])


def products_kernel(order_ref, place_ref, *refs, first, count, widths):
    n = len(widths)
    a_ref, other_ref = refs[0], refs[1]
    own_refs, g_refs, partner_refs = refs[2 : 2 + n], refs[2 + n : 2 + 2 * n], refs[2 + 2 * n : 2 + 3 * n]
    out_refs = refs[2 + 3 * n : 2 + 4 * n]
    a_buf, p_buf, g_buf, partner_buf, out_buf, in_sems, out_sems = refs[2 + 4 * n :]
    blocks, block, tokens = a_ref.shape
    rows, half = count * block, tokens // 2
    lanes = tokens // place_ref.shape[0]

    def loads(v):
        slot, w = v % 2, widths[v]
        pairs = [
            (own_refs[v].at[pl.ds(first * block, rows)], p_buf.at[slot, :, pl.ds(0, half)]),
            (other_ref.at[v, pl.ds(first * block, rows)], p_buf.at[slot, :, pl.ds(half, half)]),
            (g_refs[v], g_buf.at[slot, :, pl.ds(0, w)]),
        ]
        for j in range(count):
            pairs.append((a_ref.at[order_ref[v * blocks + first + j]], a_buf.at[slot, pl.ds(j * block, block)]))
        for k in range(place_ref.shape[0]):
            start = pl.multiple_of(place_ref[k] * lanes, lanes)
            pairs.append(
                (partner_refs[v].at[pl.ds(start, lanes)], partner_buf.at[slot, pl.ds(k * lanes, lanes), pl.ds(0, w)])
            )
        return [pltpu.make_async_copy(src, dst, in_sems.at[slot, i]) for i, (src, dst) in enumerate(pairs)]

    def store(v):
        slot = v % 2
        return pltpu.make_async_copy(out_buf.at[slot, :, pl.ds(0, widths[v])], out_refs[v], out_sems.at[slot])

    for copy in loads(0):
        copy.start()
    for v in range(n):
        slot, w = v % 2, widths[v]
        if v + 1 < n:
            for copy in loads(v + 1):
                copy.start()
        for copy in loads(v):
            copy.wait()
        if v >= 2:
            store(v - 2).wait()
        step = rows // 2
        for m in range(2):
            part = pl.ds(m * step, step)
            total = jnp.dot(a_buf[slot, part], g_buf[slot, :, :w], preferred_element_type=jnp.float32)
            total += jnp.dot(p_buf[slot, part], partner_buf[slot, :, :w], preferred_element_type=jnp.float32)
            out_buf[slot, part, :w] = total.astype(out_buf.dtype)
        store(v).start()
    for v in range(max(n - 2, 0), n):
        store(v).wait()


def products(a_blocks, own, other, g, partner, order, place, first, count):
    n = len(g)
    blocks, block, tokens = a_blocks.shape
    rows = count * block
    widths = tuple(value.shape[1] for value in g)
    widest = max(widths)
    anywhere = pl.BlockSpec(memory_space=pl.ANY)
    smem = pl.BlockSpec(memory_space=pltpu.SMEM)
    return pl.pallas_call(
        functools.partial(products_kernel, first=first, count=count, widths=widths),
        in_specs=[smem, smem] + [anywhere] * (2 + 3 * n),
        out_specs=[anywhere] * n,
        out_shape=[jax.ShapeDtypeStruct((rows, w), jnp.bfloat16) for w in widths],
        scratch_shapes=[
            pltpu.VMEM((2, rows, tokens), jnp.bfloat16),
            pltpu.VMEM((2, rows, tokens), jnp.bfloat16),
            pltpu.VMEM((2, tokens, widest), jnp.bfloat16),
            pltpu.VMEM((2, tokens, widest), jnp.bfloat16),
            pltpu.VMEM((2, rows, widest), jnp.bfloat16),
            pltpu.SemaphoreType.DMA((2, 3 + count + place.shape[0])),
            pltpu.SemaphoreType.DMA((2,)),
        ],
        compiler_params=pltpu.CompilerParams(vmem_limit_bytes=40 * 1024 * 1024),
        cost_estimate=pl.CostEstimate(
            flops=4 * rows * tokens * sum(widths),
            bytes_accessed=2 * (2 * n * rows * tokens + (2 * tokens + rows) * sum(widths)),
            transcendentals=0,
        ),
    )(order, place, a_blocks, other, *own, *g, *partner)


def pick_rows_kernel(index_ref, own_ref, below_ref, above_ref, far_top_ref, far_bottom_ref, *out_refs):
    step, steps = pl.program_id(0), pl.num_programs(0)
    lanes = own_ref.shape[2]
    half = far_top_ref.shape[0]
    for v, out_ref in enumerate(out_refs):
        b = index_ref[v * steps + step]
        for k, in_ref in enumerate((own_ref, below_ref, above_ref)):
            out_ref[:, k * lanes : (k + 1) * lanes] = in_ref[b]

        @pl.when(b < half)
        def _():
            out_ref[:, 3 * lanes :] = far_top_ref[jnp.minimum(b, half - 1)]

        @pl.when(b >= half)
        def _():
            out_ref[:, 3 * lanes :] = far_bottom_ref[jnp.maximum(b - half, 0)]


def pick_rows(pieces, index, n, block):
    rows, lanes = pieces[0].shape
    count = index.shape[0] // n
    pieces = [piece.reshape(-1, block, lanes) for piece in pieces]
    return pl.pallas_call(
        pick_rows_kernel,
        grid_spec=pltpu.PrefetchScalarGridSpec(
            num_scalar_prefetch=1,
            grid=(count,),
            in_specs=[pl.BlockSpec(piece.shape, lambda i, ref: (0, 0, 0)) for piece in pieces],
            out_specs=[pl.BlockSpec((block, 4 * lanes), lambda i, ref: (i, 0)) for _ in range(n)],
        ),
        out_shape=[jax.ShapeDtypeStruct((count * block, 4 * lanes), jnp.bfloat16) for _ in range(n)],
        compiler_params=pltpu.CompilerParams(vmem_limit_bytes=40 * 1024 * 1024),
        cost_estimate=pl.CostEstimate(
            flops=0, bytes_accessed=8 * rows * lanes + 8 * n * count * block * lanes, transcendentals=0
        ),
    )(index, *pieces)


def turn_kernel(in_ref, out_ref):
    out_ref[...] = in_ref[...].T


def turn(value):
    tokens, width = value.shape
    step = 4
    return pl.pallas_call(
        turn_kernel,
        grid=(step,),
        in_specs=[pl.BlockSpec((tokens, width // step), lambda i: (0, i))],
        out_specs=pl.BlockSpec((width // step, tokens), lambda i: (i, 0)),
        out_shape=jax.ShapeDtypeStruct((width, tokens), value.dtype),
    )(value)


def join_kernel(place_ref, *refs):
    *in_refs, out_ref = refs
    lanes = in_refs[0].shape[1]
    first_half = pl.program_id(0) < pl.num_programs(0) // 2
    for core in range(2):
        own, after, before, far_top, far_bottom = in_refs[5 * core : 5 * core + 5]

        def put(k, value):
            start = pl.multiple_of(place_ref[4 * core + k] * lanes, lanes)
            out_ref[:, pl.ds(start, lanes)] = value

        put(0, own[...])
        put(1, after[...])
        put(2, before[...])

        @pl.when(first_half)
        def _():
            put(3, far_top[...])

        @pl.when(jnp.logical_not(first_half))
        def _():
            put(3, far_bottom[...])


def join(place, pieces):
    rows, lanes = pieces[0].shape
    steps = 8
    block = rows // steps
    whole = pl.BlockSpec((block, lanes), lambda i, ref: (i, 0))
    top = pl.BlockSpec((block, lanes), lambda i, ref: (jnp.minimum(i, steps // 2 - 1), 0))
    bottom = pl.BlockSpec((block, lanes), lambda i, ref: (jnp.maximum(i - steps // 2, 0), 0))
    return pl.pallas_call(
        join_kernel,
        grid_spec=pltpu.PrefetchScalarGridSpec(
            num_scalar_prefetch=1,
            grid=(steps,),
            in_specs=[whole, whole, whole, top, bottom] * 2,
            out_specs=pl.BlockSpec((block, 8 * lanes), lambda i, ref: (i, 0)),
        ),
        out_shape=jax.ShapeDtypeStruct((rows, 8 * lanes), pieces[0].dtype),
        cost_estimate=pl.CostEstimate(flops=0, bytes_accessed=32 * rows * lanes, transcendentals=0),
    )(place, *pieces)


def gather_tokens(mine, early):
    me = lax.axis_index("seq")
    n = lax.axis_size("seq")
    up = [(i, (i + 2) % n) for i in range(n)]
    down = [(i, (i - 2) % n) for i in range(n)]
    half = mine.shape[0] // 2
    x, core = me // 2, me % 2
    place = [2 * ((x + shift) % (n // 2)) + c for c in (core, 1 - core) for shift in (0, 3, 1, 2)]
    below = lax.ppermute(mine, "seq", up)
    above = lax.ppermute(mine, "seq", down)
    below, above, place, early = lax.optimization_barrier((below, above, jnp.stack(place).astype(jnp.int32), early))
    far_top = lax.ppermute(below[:half], "seq", up)
    far_bottom = lax.ppermute(above[half:], "seq", down)
    own = [mine, below, above, far_top, far_bottom]
    other = [exchange(piece, "seq", 1) for piece in own]
    return own, other, place, early


def split_kernel(in_ref, out_ref):
    out_ref[0] = in_ref[...]


def split(value, n):
    rows, total = value.shape
    return pl.pallas_call(
        split_kernel,
        grid=(n,),
        in_specs=[pl.BlockSpec((rows, total // n), lambda i: (0, i))],
        out_specs=pl.BlockSpec((1, rows, total // n), lambda i: (i, 0, 0)),
        out_shape=jax.ShapeDtypeStruct((n, rows, total // n), value.dtype),
        cost_estimate=pl.CostEstimate(flops=0, bytes_accessed=4 * rows * total, transcendentals=0),
    )(value)


def add(a, b):
    return (a.astype(jnp.float32) + b.astype(jnp.float32)).astype(jnp.bfloat16)


def on_device(acts, grads):
    seq_count = lax.axis_size("seq")
    replica_count = lax.axis_size("dp")
    examples, local_len, width = acts.shape
    hidden = grads.shape[2]
    local = examples * local_len
    tokens = seq_count * local
    block = width // replica_count
    me = lax.axis_index("dp")

    half = replica_count // 2
    order = me ^ jnp.array([block_order(masks) for masks in ORDERS], jnp.int32)
    early = (order.reshape(-1), order[:, half:].reshape(-1))
    own, other, place, (order, sent_order) = gather_tokens(turn(acts.reshape(local, width)), early)

    pieces, own = lax.optimization_barrier((split(grads.reshape(local, hidden), seq_count), own))
    g_all = lax.all_to_all(pieces, "seq", split_axis=0, concat_axis=0, tiled=True)
    sent_rows = pick_rows(own, sent_order, len(ORDERS), block)
    other, sent_rows = lax.optimization_barrier((other, sent_rows))
    own_rows = [exchange(value, "dp", masks[0]) for value, masks in zip(sent_rows, ORDERS)]
    a_t = join(place, [*own, *other])
    a_blocks = a_t.reshape(replica_count, block, tokens)
    example = (jnp.arange(tokens) // local_len) % examples
    same = example[:, None] == example[None, :]
    act_gram = lax.dot_general(a_t, a_t, (((0,), (0,)), ((), ())), preferred_element_type=jnp.float32)
    act_gram = jnp.where(same, act_gram, 0.0)
    g_all, act_gram, own_rows = lax.optimization_barrier((g_all, act_gram, own_rows))
    g_all = g_all.reshape(tokens, -1)
    parts, low = [], 0
    for size in WIDTHS:
        parts.append(g_all[:, low : low + size])
        low += size
    partner_parts = [exchange(piece, "dp", masks[0]) for piece, masks in zip(parts, ORDERS)]
    other_rows = exchange(jnp.stack(own_rows), "seq", 1)

    gram = lax.dot_general(g_all, g_all, (((1,), (1,)), ((), ())), preferred_element_type=jnp.float32)
    rows_sum = jnp.sum(act_gram * gram, axis=1)
    partial_value = jnp.sum(rows_sum.reshape(seq_count, examples, local_len), axis=(0, 2))
    norms = jnp.sqrt(lax.psum(partial_value, "seq"))
    norms, partner_parts, other_rows = lax.optimization_barrier((norms, partner_parts, other_rows))
    partner_norms = [exchange(norms, "dp", masks[0]) for masks in ORDERS]
    factor = math.sqrt(width * hidden / (examples * replica_count))

    def scaled(piece, norm):
        clip = jnp.minimum(1.0, 1.0 / (norm + 1e-06))
        scale = jnp.tile(jnp.repeat(clip * factor, local_len), seq_count)[:, None]
        return (piece * scale).astype(jnp.bfloat16)

    g = [scaled(piece, norms) for piece in parts]
    partner_g = [scaled(piece, norm) for piece, norm in zip(partner_parts, partner_norms)]
    quarter = half // 2
    sends = products(a_blocks, own_rows, other_rows, g, partner_g, order, place, quarter, quarter)
    keeps = products(a_blocks, own_rows, other_rows, g, partner_g, order, place, 0, quarter)

    received = [exchange(send, "dp", masks[1]) for send, masks in zip(sends, ORDERS)]
    for step in (2, 3):
        rows = keeps[0].shape[0] // 2
        sends = [add(keep[rows:], value[rows:]) for keep, value in zip(keeps, received)]
        sends = lax.optimization_barrier(sends)
        sent = [exchange(send, "dp", masks[step]) for send, masks in zip(sends, ORDERS)]
        keeps = [add(keep[:rows], value[:rows]) for keep, value in zip(keeps, received)]
        received = sent
    outs = [add(keep, value) for keep, value in zip(keeps, received)]
    return (jnp.concatenate(outs, axis=1), norms)


def solution(mesh):
    return jax.shard_map(
        on_device,
        mesh=mesh,
        in_specs=(P("dp", "seq", None), P("dp", "seq", None)),
        out_specs=(P("dp", "seq"), P("dp")),
        check_vma=False,
    )
```

```python
import functools
import math

import jax
import jax.numpy as jnp
from jax import lax
from jax.experimental import pallas as pl
from jax.experimental.pallas import tpu as pltpu
from jax.sharding import PartitionSpec as P

ORDERS = ((4, 12, 1, 3), (12, 4, 3, 1), (1, 3, 4, 12), (3, 1, 12, 4))
WIDTHS = (640, 640, 512, 512)


def block_order(masks):
    order = [0]
    for mask in reversed(masks):
        order = order + [mask ^ k for k in order]
    return order


def exchange(value, axis, mask):
    return lax.ppermute(value, axis, [(i, i ^ mask) for i in range(lax.axis_size(axis))])


def products_kernel(
    order_ref, place_ref, scale_ref, *refs, groups, first, count, widths, examples, own, partner, base
):
    n = len(groups)
    refs = list(refs)

    def take(k):
        taken = refs[:k]
        del refs[:k]
        return taken

    if own:
        (a_ref,) = take(1)
        g_refs = take(n)
    if partner:
        own_refs, other_refs, partner_refs = take(n), take(n), take(n)
    if base:
        base_refs = take(n)
    out_refs = take(n)
    lhs, rhs, out_buf, in_sems, out_sems = refs
    depth = lhs.shape[2]
    rows = lhs.shape[1]
    block = rows // count
    tokens = depth // (own + partner)
    lanes = tokens // place_ref.shape[0]
    blocks = order_ref.shape[0] // len(widths)
    slab = lanes // examples

    def loads(i):
        v, slot = groups[i], i % 2
        w = widths[v]
        low = widths[v - 1] if v % 2 else 0
        pairs = []
        start = 0
        if own:
            pairs.append((g_refs[i].at[:, pl.ds(low, w)], rhs.at[slot, pl.ds(0, tokens), pl.ds(0, w)]))
            for j in range(count):
                pairs.append(
                    (
                        a_ref.at[order_ref[v * blocks + first + j]],
                        lhs.at[slot, pl.ds(j * block, block), pl.ds(0, tokens)],
                    )
                )
            start = tokens
        if partner:
            for k, ref in enumerate((own_refs[i], other_refs[i])):
                size = ref.shape[1]
                pairs.append(
                    (ref.at[pl.ds(first * block, rows)], lhs.at[slot, :, pl.ds(start + k * size, size)])
                )
            for k in range(place_ref.shape[0]):
                source = pl.multiple_of(place_ref[k] * lanes, lanes)
                pairs.append(
                    (
                        partner_refs[i].at[pl.ds(source, lanes)],
                        rhs.at[slot, pl.ds(start + k * lanes, lanes), pl.ds(0, w)],
                    )
                )
        if base:
            pairs.append((base_refs[i], out_buf.at[slot, :, pl.ds(0, w)]))
        return [pltpu.make_async_copy(src, dst, in_sems.at[slot, k]) for k, (src, dst) in enumerate(pairs)]

    def store(i):
        slot = i % 2
        return pltpu.make_async_copy(out_buf.at[slot, :, pl.ds(0, widths[groups[i]])], out_refs[i], out_sems.at[slot])

    for copy in loads(0):
        copy.start()
    for i in range(n):
        v, slot = groups[i], i % 2
        w = widths[v]
        if i + 1 < n:
            if i >= 1:
                store(i - 1).wait()
            for copy in loads(i + 1):
                copy.start()
        for copy in loads(i):
            copy.wait()
        for r in range(depth // slab):
            number = r % examples if own and r < tokens // slab else (v + 1) * examples + r % examples
            part = pl.ds(r * slab, slab)
            value = rhs[slot, part, :w].astype(jnp.float32) * scale_ref[number]
            rhs[slot, part, :w] = value.astype(rhs.dtype)
        step = rows // 2
        for m in range(2):
            part = pl.ds(m * step, step)
            total = jnp.dot(lhs[slot, part], rhs[slot, :, :w], preferred_element_type=jnp.float32)
            if base:
                total += out_buf[slot, part, :w].astype(jnp.float32)
            out_buf[slot, part, :w] = total.astype(out_buf.dtype)
        store(i).start()
    for i in range(max(n - 2, 0), n):
        store(i).wait()


def products(
    groups, order, place, scale, examples, first, count, own=None, partner=None, base=None, hint=1
):
    n = len(groups)
    operands, pieces = [], 0
    if own is not None:
        a_blocks, g = own
        operands += [a_blocks, *[g[v // 2] for v in groups]]
        blocks, block, tokens = a_blocks.shape
        pieces += 1 + count
    if partner is not None:
        for values in partner:
            operands += [values[v] for v in groups]
        tokens = partner[2][0].shape[0]
        block = partner[0][0].shape[0] // (2 * count)
        pieces += 2 + place.shape[0]
    if base is not None:
        operands += [base[v] for v in groups]
        pieces += 1
    rows = count * block
    depth = tokens * ((own is not None) + (partner is not None))
    widths = tuple(WIDTHS[v] for v in groups)
    widest = max(widths)
    anywhere = pl.BlockSpec(memory_space=pl.ANY)
    smem = pl.BlockSpec(memory_space=pltpu.SMEM)
    return pl.pallas_call(
        functools.partial(
            products_kernel,
            groups=groups,
            first=first,
            count=count,
            widths=WIDTHS,
            examples=examples,
            own=own is not None,
            partner=partner is not None,
            base=base is not None,
        ),
        in_specs=[smem, smem, smem] + [anywhere] * len(operands),
        out_specs=[anywhere] * n,
        out_shape=[jax.ShapeDtypeStruct((rows, w), jnp.bfloat16) for w in widths],
        scratch_shapes=[
            pltpu.VMEM((2, rows, depth), jnp.bfloat16),
            pltpu.VMEM((2, depth, widest), jnp.bfloat16),
            pltpu.VMEM((2, rows, widest), jnp.bfloat16),
            pltpu.SemaphoreType.DMA((2, pieces)),
            pltpu.SemaphoreType.DMA((2,)),
        ],
        compiler_params=pltpu.CompilerParams(vmem_limit_bytes=40 * 1024 * 1024),
        cost_estimate=pl.CostEstimate(
            flops=int(hint * 2 * rows * depth * sum(widths)),
            bytes_accessed=int(hint * 2 * (n * rows * depth + (depth + rows) * sum(widths))),
            transcendentals=0,
        ),
    )(order, place, scale, *operands)


def pick_near_kernel(index_ref, *refs, sources):
    step, steps = pl.program_id(0), pl.num_programs(0)
    in_refs, out_refs = refs[:sources], refs[sources:]
    lanes = in_refs[0].shape[2]
    for v, out_ref in enumerate(out_refs):
        for k, in_ref in enumerate(in_refs):
            out_ref[:, k * lanes : (k + 1) * lanes] = in_ref[index_ref[v * steps + step]]


def pick_near(pieces, index, n, block):
    lanes = pieces[0].shape[1]
    count = index.shape[0] // n
    pieces = [piece.reshape(-1, block, lanes) for piece in pieces]
    total = (len(pieces) + 1) * lanes
    return pl.pallas_call(
        functools.partial(pick_near_kernel, sources=len(pieces)),
        grid_spec=pltpu.PrefetchScalarGridSpec(
            num_scalar_prefetch=1,
            grid=(count,),
            in_specs=[pl.BlockSpec(piece.shape, lambda i, ref: (0, 0, 0)) for piece in pieces],
            out_specs=[pl.BlockSpec((block, total), lambda i, ref: (i, 0)) for _ in range(n)],
        ),
        out_shape=[jax.ShapeDtypeStruct((count * block, total), jnp.bfloat16) for _ in range(n)],
        compiler_params=pltpu.CompilerParams(vmem_limit_bytes=40 * 1024 * 1024),
        cost_estimate=pl.CostEstimate(flops=0, bytes_accessed=4 * n * count * block * total, transcendentals=0),
    )(index, *pieces)


def pick_far_kernel(index_ref, top_ref, bottom_ref, *refs):
    step, steps = pl.program_id(0), pl.num_programs(0)
    half = top_ref.shape[0]
    out_refs = refs[len(refs) // 2 :]
    for v, out_ref in enumerate(out_refs):
        b = index_ref[v * steps + step]

        @pl.when(b < half)
        def _():
            out_ref[...] = top_ref[jnp.minimum(b, half - 1)]

        @pl.when(b >= half)
        def _():
            out_ref[...] = bottom_ref[jnp.maximum(b - half, 0)]


def pick_far(top, bottom, index, near, block):
    lanes = top.shape[1]
    n = len(near)
    count = index.shape[0] // n
    last = near[0].shape[1] // lanes - 1
    halves = [piece.reshape(-1, block, lanes) for piece in (top, bottom)]
    return pl.pallas_call(
        pick_far_kernel,
        grid_spec=pltpu.PrefetchScalarGridSpec(
            num_scalar_prefetch=1,
            grid=(count,),
            in_specs=[pl.BlockSpec(piece.shape, lambda i, ref: (0, 0, 0)) for piece in halves]
            + [pl.BlockSpec(memory_space=pl.ANY)] * n,
            out_specs=[pl.BlockSpec((block, lanes), lambda i, ref: (i, last)) for _ in range(n)],
        ),
        out_shape=[jax.ShapeDtypeStruct(value.shape, value.dtype) for value in near],
        input_output_aliases={3 + v: v for v in range(n)},
        compiler_params=pltpu.CompilerParams(vmem_limit_bytes=40 * 1024 * 1024),
        cost_estimate=pl.CostEstimate(flops=0, bytes_accessed=4 * n * count * block * lanes, transcendentals=0),
    )(index, *halves, *near)


def turn_kernel(in_ref, out_ref):
    out_ref[...] = in_ref[...].T


def turn(value):
    tokens, width = value.shape
    step = 4
    return pl.pallas_call(
        turn_kernel,
        grid=(step,),
        in_specs=[pl.BlockSpec((tokens, width // step), lambda i: (0, i))],
        out_specs=pl.BlockSpec((width // step, tokens), lambda i: (i, 0)),
        out_shape=jax.ShapeDtypeStruct((width, tokens), value.dtype),
    )(value)


def join_kernel(place_ref, *refs):
    *in_refs, out_ref = refs
    lanes = in_refs[0].shape[1]
    first_half = pl.program_id(0) < pl.num_programs(0) // 2
    for core in range(2):
        own, after, before, far_top, far_bottom = in_refs[5 * core : 5 * core + 5]

        def put(k, value):
            start = pl.multiple_of(place_ref[4 * core + k] * lanes, lanes)
            out_ref[:, pl.ds(start, lanes)] = value

        put(0, own[...])
        put(1, after[...])
        put(2, before[...])

        @pl.when(first_half)
        def _():
            put(3, far_top[...])

        @pl.when(jnp.logical_not(first_half))
        def _():
            put(3, far_bottom[...])


def join(place, pieces):
    rows, lanes = pieces[0].shape
    steps = 8
    block = rows // steps
    whole = pl.BlockSpec((block, lanes), lambda i, ref: (i, 0))
    top = pl.BlockSpec((block, lanes), lambda i, ref: (jnp.minimum(i, steps // 2 - 1), 0))
    bottom = pl.BlockSpec((block, lanes), lambda i, ref: (jnp.maximum(i - steps // 2, 0), 0))
    return pl.pallas_call(
        join_kernel,
        grid_spec=pltpu.PrefetchScalarGridSpec(
            num_scalar_prefetch=1,
            grid=(steps,),
            in_specs=[whole, whole, whole, top, bottom] * 2,
            out_specs=pl.BlockSpec((block, 8 * lanes), lambda i, ref: (i, 0)),
        ),
        out_shape=jax.ShapeDtypeStruct((rows, 8 * lanes), pieces[0].dtype),
        cost_estimate=pl.CostEstimate(flops=0, bytes_accessed=32 * rows * lanes, transcendentals=0),
    )(place, *pieces)


def split_kernel(in_ref, *out_refs):
    low = 0
    for out_ref in out_refs:
        size = out_ref.shape[2]
        out_ref[0] = in_ref[:, low : low + size]
        low += size


def split(value, n, widths):
    rows, total = value.shape
    return pl.pallas_call(
        split_kernel,
        grid=(n,),
        in_specs=[pl.BlockSpec((rows, total // n), lambda i: (0, i))],
        out_specs=[pl.BlockSpec((1, rows, w), lambda i: (i, 0, 0)) for w in widths],
        out_shape=[jax.ShapeDtypeStruct((n, rows, w), value.dtype) for w in widths],
        cost_estimate=pl.CostEstimate(flops=0, bytes_accessed=4 * rows * total, transcendentals=0),
    )(value)


def add(a, b):
    return (a.astype(jnp.float32) + b.astype(jnp.float32)).astype(jnp.bfloat16)


def on_device(acts, grads):
    seq_count = lax.axis_size("seq")
    replica_count = lax.axis_size("dp")
    examples, local_len, width = acts.shape
    hidden = grads.shape[2]
    local = examples * local_len
    tokens = seq_count * local
    block = width // replica_count
    me = lax.axis_index("dp")

    me_seq = lax.axis_index("seq")
    x, core = me_seq // 2, me_seq % 2
    place = [2 * ((x + shift) % (seq_count // 2)) + c for c in (core, 1 - core) for shift in (0, 3, 1, 2)]
    half = replica_count // 2
    order = me ^ jnp.array([block_order(masks) for masks in ORDERS], jnp.int32)
    tables = (jnp.stack(place).astype(jnp.int32), order.reshape(-1), order[:, half:].reshape(-1))
    up = [(i, (i + 2) % seq_count) for i in range(seq_count)]
    down = [(i, (i - 2) % seq_count) for i in range(seq_count)]
    groups = len(ORDERS)

    mine = turn(acts.reshape(local, width))
    below = lax.ppermute(mine, "seq", up)
    above = lax.ppermute(mine, "seq", down)
    below, above, pieces, (place, order, sent_order) = lax.optimization_barrier(
        (below, above, split(grads.reshape(local, hidden), seq_count, (sum(WIDTHS[:2]), sum(WIDTHS[2:]))), tables)
    )
    middle = width // 2
    far_top = lax.ppermute(below[:middle], "seq", up)
    far_bottom = lax.ppermute(above[middle:], "seq", down)
    near = pick_near([mine, below, above], sent_order, groups, block)
    pieces, far_top, far_bottom, near = lax.optimization_barrier((pieces, far_top, far_bottom, near))
    g = [lax.all_to_all(piece, "seq", split_axis=0, concat_axis=0, tiled=True) for piece in pieces]
    g = [value.reshape(tokens, -1) for value in g]

    sent_rows = pick_far(far_top, far_bottom, sent_order, near, block)
    own_rows = [exchange(value, "dp", masks[0]) for value, masks in zip(sent_rows, ORDERS)]

    own = [mine, below, above, far_top, far_bottom]
    a_t = join(place, own + [exchange(piece, "seq", 1) for piece in own])
    a_blocks = a_t.reshape(replica_count, block, tokens)
    example = (jnp.arange(tokens) // local_len) % examples
    same = example[:, None] == example[None, :]
    act_gram = lax.dot_general(a_t, a_t, (((0,), (0,)), ((), ())), preferred_element_type=jnp.float32)
    act_gram = jnp.where(same, act_gram, 0.0)

    def pairing(value):
        gram = lax.dot_general(value, value, (((1,), (1,)), ((), ())), preferred_element_type=jnp.float32)
        return jnp.sum(act_gram * gram, axis=1)

    rows_sum = pairing(g[0])

    def columns_of(v, value):
        low = WIDTHS[v - 1] if v % 2 else 0
        return value[:, low : low + WIDTHS[v]]

    parts = [columns_of(v, g[0]) for v in (0, 1)]
    rows_sum, parts, g, own_rows = lax.optimization_barrier((rows_sum, parts, g, own_rows))
    parts += [columns_of(v, g[1]) for v in (2, 3)]
    parts, g = lax.optimization_barrier((parts, g))
    partner = [exchange(piece, "dp", masks[0]) for piece, masks in zip(parts, ORDERS)]
    other_rows = [exchange(own_rows[0], "seq", 1)]
    rows_sum = rows_sum + pairing(g[1])
    rows_sum, other_rows[0], own_rows[1] = lax.optimization_barrier((rows_sum, other_rows[0], own_rows[1]))
    other_rows.append(exchange(own_rows[1], "seq", 1))
    rows_sum, other_rows[1] = lax.optimization_barrier((rows_sum, other_rows[1]))
    partial_value = jnp.sum(rows_sum.reshape(seq_count, examples, local_len), axis=(0, 2))
    for mask in (1, 2, 6):
        partial_value = partial_value + exchange(partial_value, "seq", mask)
    norms = jnp.sqrt(partial_value)
    factor = math.sqrt(width * hidden / (examples * replica_count))

    def scale_of(norm):
        return jnp.minimum(1.0, 1.0 / (norm + 1e-06)) * factor

    quarter = half // 2
    make = functools.partial(products, order=order, place=place, examples=examples, count=quarter)
    scale = scale_of(norms)
    base = make((0, 1, 2, 3), scale=scale, first=quarter, own=(a_blocks, g), hint=0.02)
    norms, scale, base, partner, other_rows, own_rows = lax.optimization_barrier(
        (norms, scale, base, partner, other_rows, own_rows)
    )
    other_norms = [exchange(norms, "dp", masks[0]) for masks in ORDERS]
    other_rows += [exchange(value, "seq", 1) for value in own_rows[2:]]
    scale = jnp.concatenate([scale] + [scale_of(norm) for norm in other_norms[:2]])
    sends = make((0, 1), scale=scale, first=quarter, partner=(own_rows, other_rows, partner), base=base)
    sends, other_rows, other_norms, scale = lax.optimization_barrier((sends, other_rows, other_norms, scale))
    scale = jnp.concatenate([scale] + [scale_of(norm) for norm in other_norms[2:]])
    sends = [
        *sends,
        *make((2, 3), scale=scale, first=quarter, partner=(own_rows, other_rows, partner), base=base),
    ]
    keeps = make(
        (0, 1, 2, 3), scale=scale, first=0, own=(a_blocks, g), partner=(own_rows, other_rows, partner)
    )

    received = [exchange(send, "dp", masks[1]) for send, masks in zip(sends, ORDERS)]
    for step in (2, 3):
        rows = keeps[0].shape[0] // 2
        sends = [add(keep[rows:], value[rows:]) for keep, value in zip(keeps, received)]
        sends = lax.optimization_barrier(sends)
        sent = [exchange(send, "dp", masks[step]) for send, masks in zip(sends, ORDERS)]
        keeps = [add(keep[:rows], value[:rows]) for keep, value in zip(keeps, received)]
        received = sent
    outs = [add(keep, value) for keep, value in zip(keeps, received)]
    return (jnp.concatenate(outs, axis=1), norms)


def solution(mesh):
    return jax.shard_map(
        on_device,
        mesh=mesh,
        in_specs=(P("dp", "seq", None), P("dp", "seq", None)),
        out_specs=(P("dp", "seq"), P("dp")),
        check_vma=False,
    )
```

```python
import functools
import math

import jax
import jax.numpy as jnp
from jax import lax
from jax.experimental import pallas as pl
from jax.experimental.pallas import tpu as pltpu
from jax.sharding import PartitionSpec as P

ORDERS = ((4, 12, 1, 3), (12, 4, 3, 1), (1, 3, 4, 12), (3, 1, 12, 4))
WIDTHS = (640, 640, 512, 512)


def block_order(masks):
    order = [0]
    for mask in reversed(masks):
        order = order + [mask ^ k for k in order]
    return order


def exchange(value, axis, mask):
    return lax.ppermute(value, axis, [(i, i ^ mask) for i in range(lax.axis_size(axis))])


def products_kernel(
    order_ref, place_ref, scale_ref, *refs, groups, first, count, widths, examples, own, partner, base
):
    n = len(groups)
    refs = list(refs)

    def take(k):
        taken = refs[:k]
        del refs[:k]
        return taken

    if own:
        (a_ref,) = take(1)
        g_refs = take(n)
    if partner:
        own_refs, other_refs, partner_refs = take(n), take(n), take(n)
    if base:
        base_refs = take(n)
    out_refs = take(n)
    lhs, rhs, out_buf, in_sems, out_sems = refs
    depth = lhs.shape[2]
    rows = lhs.shape[1]
    block = rows // count
    tokens = depth // (own + partner)
    lanes = tokens // place_ref.shape[0]
    blocks = order_ref.shape[0] // len(widths)
    slab = lanes // examples

    def loads(i):
        v, slot = groups[i], i % 2
        w = widths[v]
        low = widths[v - 1] if v % 2 else 0
        pairs = []
        start = 0
        if own:
            pairs.append((g_refs[i].at[:, pl.ds(low, w)], rhs.at[slot, pl.ds(0, tokens), pl.ds(0, w)]))
            for j in range(count):
                pairs.append(
                    (
                        a_ref.at[order_ref[v * blocks + first + j]],
                        lhs.at[slot, pl.ds(j * block, block), pl.ds(0, tokens)],
                    )
                )
            start = tokens
        if partner:
            for k, ref in enumerate((own_refs[i], other_refs[i])):
                size = ref.shape[1]
                pairs.append(
                    (ref.at[pl.ds(first * block, rows)], lhs.at[slot, :, pl.ds(start + k * size, size)])
                )
            for k in range(place_ref.shape[0]):
                source = pl.multiple_of(place_ref[k] * lanes, lanes)
                pairs.append(
                    (
                        partner_refs[i].at[pl.ds(source, lanes)],
                        rhs.at[slot, pl.ds(start + k * lanes, lanes), pl.ds(0, w)],
                    )
                )
        if base:
            pairs.append((base_refs[i], out_buf.at[slot, :, pl.ds(0, w)]))
        return [pltpu.make_async_copy(src, dst, in_sems.at[slot, k]) for k, (src, dst) in enumerate(pairs)]

    def store(i):
        slot = i % 2
        return pltpu.make_async_copy(out_buf.at[slot, :, pl.ds(0, widths[groups[i]])], out_refs[i], out_sems.at[slot])

    for copy in loads(0):
        copy.start()
    for i in range(n):
        v, slot = groups[i], i % 2
        w = widths[v]
        if i + 1 < n:
            if i >= 1:
                store(i - 1).wait()
            for copy in loads(i + 1):
                copy.start()
        for copy in loads(i):
            copy.wait()
        for r in range(depth // slab):
            whose = order_ref[v * blocks + (0 if own and r < tokens // slab else blocks // 2)]
            part = pl.ds(r * slab, slab)
            value = rhs[slot, part, :w].astype(jnp.float32) * scale_ref[whose * examples + r % examples]
            rhs[slot, part, :w] = value.astype(rhs.dtype)
        step = rows // 2
        for m in range(2):
            part = pl.ds(m * step, step)
            total = jnp.dot(lhs[slot, part], rhs[slot, :, :w], preferred_element_type=jnp.float32)
            if base:
                total += out_buf[slot, part, :w].astype(jnp.float32)
            out_buf[slot, part, :w] = total.astype(out_buf.dtype)
        store(i).start()
    for i in range(max(n - 2, 0), n):
        store(i).wait()


def products(
    groups, order, place, scale, examples, first, count, own=None, partner=None, base=None, hint=1
):
    n = len(groups)
    operands, pieces = [], 0
    if own is not None:
        a_blocks, g = own
        operands += [a_blocks, *[g[v // 2] for v in groups]]
        blocks, block, tokens = a_blocks.shape
        pieces += 1 + count
    if partner is not None:
        for values in partner:
            operands += [values[v] for v in groups]
        tokens = partner[2][0].shape[0]
        block = partner[0][0].shape[0] // (2 * count)
        pieces += 2 + place.shape[0]
    if base is not None:
        operands += [base[v] for v in groups]
        pieces += 1
    rows = count * block
    depth = tokens * ((own is not None) + (partner is not None))
    widths = tuple(WIDTHS[v] for v in groups)
    widest = max(widths)
    anywhere = pl.BlockSpec(memory_space=pl.ANY)
    smem = pl.BlockSpec(memory_space=pltpu.SMEM)
    return pl.pallas_call(
        functools.partial(
            products_kernel,
            groups=groups,
            first=first,
            count=count,
            widths=WIDTHS,
            examples=examples,
            own=own is not None,
            partner=partner is not None,
            base=base is not None,
        ),
        in_specs=[smem, smem, smem] + [anywhere] * len(operands),
        out_specs=[anywhere] * n,
        out_shape=[jax.ShapeDtypeStruct((rows, w), jnp.bfloat16) for w in widths],
        scratch_shapes=[
            pltpu.VMEM((2, rows, depth), jnp.bfloat16),
            pltpu.VMEM((2, depth, widest), jnp.bfloat16),
            pltpu.VMEM((2, rows, widest), jnp.bfloat16),
            pltpu.SemaphoreType.DMA((2, pieces)),
            pltpu.SemaphoreType.DMA((2,)),
        ],
        compiler_params=pltpu.CompilerParams(vmem_limit_bytes=58 * 1024 * 1024),
        cost_estimate=pl.CostEstimate(
            flops=int(hint * 2 * rows * depth * sum(widths)),
            bytes_accessed=int(hint * 2 * (n * rows * depth + (depth + rows) * sum(widths))),
            transcendentals=0,
        ),
    )(order, place, scale, *operands)


def pick_near_kernel(index_ref, *refs, sources):
    step, steps = pl.program_id(0), pl.num_programs(0)
    in_refs, out_refs = refs[:sources], refs[sources:]
    lanes = in_refs[0].shape[2]
    for v, out_ref in enumerate(out_refs):
        for k, in_ref in enumerate(in_refs):
            out_ref[:, k * lanes : (k + 1) * lanes] = in_ref[index_ref[v * steps + step]]


def pick_near(pieces, index, n, block):
    lanes = pieces[0].shape[1]
    count = index.shape[0] // n
    pieces = [piece.reshape(-1, block, lanes) for piece in pieces]
    total = (len(pieces) + 1) * lanes
    return pl.pallas_call(
        functools.partial(pick_near_kernel, sources=len(pieces)),
        grid_spec=pltpu.PrefetchScalarGridSpec(
            num_scalar_prefetch=1,
            grid=(count,),
            in_specs=[pl.BlockSpec(piece.shape, lambda i, ref: (0, 0, 0)) for piece in pieces],
            out_specs=[pl.BlockSpec((block, total), lambda i, ref: (i, 0)) for _ in range(n)],
        ),
        out_shape=[jax.ShapeDtypeStruct((count * block, total), jnp.bfloat16) for _ in range(n)],
        compiler_params=pltpu.CompilerParams(vmem_limit_bytes=40 * 1024 * 1024),
        cost_estimate=pl.CostEstimate(flops=0, bytes_accessed=4 * n * count * block * total, transcendentals=0),
    )(index, *pieces)


def pick_far_kernel(index_ref, top_ref, bottom_ref, *refs):
    step, steps = pl.program_id(0), pl.num_programs(0)
    half = top_ref.shape[0]
    out_refs = refs[len(refs) // 2 :]
    for v, out_ref in enumerate(out_refs):
        b = index_ref[v * steps + step]

        @pl.when(b < half)
        def _():
            out_ref[...] = top_ref[jnp.minimum(b, half - 1)]

        @pl.when(b >= half)
        def _():
            out_ref[...] = bottom_ref[jnp.maximum(b - half, 0)]


def pick_far(top, bottom, index, near, block):
    lanes = top.shape[1]
    n = len(near)
    count = index.shape[0] // n
    last = near[0].shape[1] // lanes - 1
    halves = [piece.reshape(-1, block, lanes) for piece in (top, bottom)]
    return pl.pallas_call(
        pick_far_kernel,
        grid_spec=pltpu.PrefetchScalarGridSpec(
            num_scalar_prefetch=1,
            grid=(count,),
            in_specs=[pl.BlockSpec(piece.shape, lambda i, ref: (0, 0, 0)) for piece in halves]
            + [pl.BlockSpec(memory_space=pl.ANY)] * n,
            out_specs=[pl.BlockSpec((block, lanes), lambda i, ref: (i, last)) for _ in range(n)],
        ),
        out_shape=[jax.ShapeDtypeStruct(value.shape, value.dtype) for value in near],
        input_output_aliases={3 + v: v for v in range(n)},
        compiler_params=pltpu.CompilerParams(vmem_limit_bytes=40 * 1024 * 1024),
        cost_estimate=pl.CostEstimate(flops=0, bytes_accessed=4 * n * count * block * lanes, transcendentals=0),
    )(index, *halves, *near)


def turn_kernel(in_ref, out_ref):
    out_ref[...] = in_ref[...].T


def turn(value):
    tokens, width = value.shape
    step = 4
    return pl.pallas_call(
        turn_kernel,
        grid=(step,),
        in_specs=[pl.BlockSpec((tokens, width // step), lambda i: (0, i))],
        out_specs=pl.BlockSpec((width // step, tokens), lambda i: (i, 0)),
        out_shape=jax.ShapeDtypeStruct((width, tokens), value.dtype),
    )(value)


def join_kernel(place_ref, *refs):
    *in_refs, out_ref = refs
    lanes = in_refs[0].shape[1]
    first_half = pl.program_id(0) < pl.num_programs(0) // 2
    for core in range(2):
        own, after, before, far_top, far_bottom = in_refs[5 * core : 5 * core + 5]

        def put(k, value):
            start = pl.multiple_of(place_ref[4 * core + k] * lanes, lanes)
            out_ref[:, pl.ds(start, lanes)] = value

        put(0, own[...])
        put(1, after[...])
        put(2, before[...])

        @pl.when(first_half)
        def _():
            put(3, far_top[...])

        @pl.when(jnp.logical_not(first_half))
        def _():
            put(3, far_bottom[...])


def join(place, pieces):
    rows, lanes = pieces[0].shape
    steps = 8
    block = rows // steps
    whole = pl.BlockSpec((block, lanes), lambda i, ref: (i, 0))
    top = pl.BlockSpec((block, lanes), lambda i, ref: (jnp.minimum(i, steps // 2 - 1), 0))
    bottom = pl.BlockSpec((block, lanes), lambda i, ref: (jnp.maximum(i - steps // 2, 0), 0))
    return pl.pallas_call(
        join_kernel,
        grid_spec=pltpu.PrefetchScalarGridSpec(
            num_scalar_prefetch=1,
            grid=(steps,),
            in_specs=[whole, whole, whole, top, bottom] * 2,
            out_specs=pl.BlockSpec((block, 8 * lanes), lambda i, ref: (i, 0)),
        ),
        out_shape=jax.ShapeDtypeStruct((rows, 8 * lanes), pieces[0].dtype),
        cost_estimate=pl.CostEstimate(flops=0, bytes_accessed=32 * rows * lanes, transcendentals=0),
    )(place, *pieces)


def split_kernel(in_ref, *out_refs):
    low = 0
    for out_ref in out_refs:
        size = out_ref.shape[2]
        out_ref[0] = in_ref[:, low : low + size]
        low += size


def split(value, n, widths):
    rows, total = value.shape
    return pl.pallas_call(
        split_kernel,
        grid=(n,),
        in_specs=[pl.BlockSpec((rows, total // n), lambda i: (0, i))],
        out_specs=[pl.BlockSpec((1, rows, w), lambda i: (i, 0, 0)) for w in widths],
        out_shape=[jax.ShapeDtypeStruct((n, rows, w), value.dtype) for w in widths],
        cost_estimate=pl.CostEstimate(flops=0, bytes_accessed=4 * rows * total, transcendentals=0),
    )(value)


def add(a, b):
    return (a.astype(jnp.float32) + b.astype(jnp.float32)).astype(jnp.bfloat16)


def on_device(acts, grads):
    seq_count = lax.axis_size("seq")
    replica_count = lax.axis_size("dp")
    examples, local_len, width = acts.shape
    hidden = grads.shape[2]
    local = examples * local_len
    tokens = seq_count * local
    block = width // replica_count
    me = lax.axis_index("dp")

    me_seq = lax.axis_index("seq")
    x, core = me_seq // 2, me_seq % 2
    place = [2 * ((x + shift) % (seq_count // 2)) + c for c in (core, 1 - core) for shift in (0, 3, 1, 2)]
    half = replica_count // 2
    order = me ^ jnp.array([block_order(masks) for masks in ORDERS], jnp.int32)
    tables = (jnp.stack(place).astype(jnp.int32), order.reshape(-1), order[:, half:].reshape(-1))
    up = [(i, (i + 2) % seq_count) for i in range(seq_count)]
    down = [(i, (i - 2) % seq_count) for i in range(seq_count)]
    groups = len(ORDERS)

    mine = turn(acts.reshape(local, width))
    below = lax.ppermute(mine, "seq", up)
    above = lax.ppermute(mine, "seq", down)
    below, above, pieces, (place, order, sent_order) = lax.optimization_barrier(
        (below, above, split(grads.reshape(local, hidden), seq_count, (sum(WIDTHS[:2]), sum(WIDTHS[2:]))), tables)
    )
    middle = width // 2
    far_top = lax.ppermute(below[:middle], "seq", up)
    far_bottom = lax.ppermute(above[middle:], "seq", down)
    near = pick_near([mine, below, above], sent_order, groups, block)
    pieces, far_top, far_bottom, near = lax.optimization_barrier((pieces, far_top, far_bottom, near))
    g = [lax.all_to_all(piece, "seq", split_axis=0, concat_axis=0, tiled=True) for piece in pieces]
    g = [value.reshape(tokens, -1) for value in g]

    sent_rows = pick_far(far_top, far_bottom, sent_order, near, block)
    own_rows = [exchange(value, "dp", masks[0]) for value, masks in zip(sent_rows, ORDERS)]

    own = [mine, below, above, far_top, far_bottom]
    a_t = join(place, own + [exchange(piece, "seq", 1) for piece in own])
    a_blocks = a_t.reshape(replica_count, block, tokens)
    example = (jnp.arange(tokens) // local_len) % examples
    same = example[:, None] == example[None, :]
    act_gram = lax.dot_general(a_t, a_t, (((0,), (0,)), ((), ())), preferred_element_type=jnp.float32)
    act_gram = jnp.where(same, act_gram, 0.0)

    def pairing(value):
        gram = lax.dot_general(value, value, (((1,), (1,)), ((), ())), preferred_element_type=jnp.float32)
        return jnp.sum(act_gram * gram, axis=1)

    rows_sum = pairing(g[0])

    def columns_of(v, value):
        low = WIDTHS[v - 1] if v % 2 else 0
        return value[:, low : low + WIDTHS[v]]

    parts = [columns_of(v, g[0]) for v in (0, 1)]
    rows_sum, parts, g, own_rows = lax.optimization_barrier((rows_sum, parts, g, own_rows))
    parts += [columns_of(v, g[1]) for v in (2, 3)]
    parts, g = lax.optimization_barrier((parts, g))
    partner = [exchange(piece, "dp", masks[0]) for piece, masks in zip(parts, ORDERS)]
    other_rows = [exchange(own_rows[0], "seq", 1)]
    rows_sum = rows_sum + pairing(g[1])
    rows_sum, other_rows[0], own_rows[1] = lax.optimization_barrier((rows_sum, other_rows[0], own_rows[1]))
    other_rows.append(exchange(own_rows[1], "seq", 1))
    rows_sum, other_rows[1] = lax.optimization_barrier((rows_sum, other_rows[1]))
    partial_value = jnp.sum(rows_sum.reshape(seq_count, examples, local_len), axis=(0, 2))
    for mask in (1, 2, 6):
        partial_value = partial_value + exchange(partial_value, "seq", mask)
    norms = jnp.sqrt(partial_value)
    factor = math.sqrt(width * hidden / (examples * replica_count))

    def scale_of(norm):
        return jnp.minimum(1.0, 1.0 / (norm + 1e-06)) * factor

    quarter = half // 2
    make = functools.partial(products, order=order, place=place, examples=examples, count=quarter)
    known = jnp.broadcast_to(jnp.pad(norms, (0, 128 - examples))[None, None], (replica_count, 8, 128))
    known = lax.all_to_all(known, "dp", split_axis=0, concat_axis=0, tiled=True)
    scale = jnp.tile(scale_of(norms), replica_count)
    base = make((0, 1, 2, 3), scale=scale, first=quarter, own=(a_blocks, g), hint=0.02)
    known, base, partner, other_rows, own_rows = lax.optimization_barrier(
        (known, base, partner, other_rows, own_rows)
    )
    other_rows += [exchange(value, "seq", 1) for value in own_rows[2:]]
    scale = scale_of(known[:, 0, :examples].reshape(-1))
    sends = make((0, 1), scale=scale, first=quarter, partner=(own_rows, other_rows, partner), base=base)
    sends, other_rows = lax.optimization_barrier((sends, other_rows))
    theirs = (own_rows, other_rows, partner)
    sends = [*sends, *make((2, 3), scale=scale, first=quarter, partner=theirs, base=base)]
    keeps = make((0, 1, 2, 3), scale=scale, first=0, own=(a_blocks, g), partner=theirs, hint=0.02)

    received = [exchange(send, "dp", masks[1]) for send, masks in zip(sends, ORDERS)]
    for step in (2, 3):
        rows = keeps[0].shape[0] // 2
        sends = [add(keeps[v][rows:], received[v][rows:]) for v in (0, 1)]
        sends, received[2:] = lax.optimization_barrier((sends, received[2:]))
        sends += [add(keeps[v][rows:], received[v][rows:]) for v in (2, 3)]
        sends = lax.optimization_barrier(sends)
        sent = [exchange(send, "dp", masks[step]) for send, masks in zip(sends, ORDERS)]
        keeps = [add(keep[:rows], value[:rows]) for keep, value in zip(keeps, received)]
        received = sent
    outs = [add(keep, value) for keep, value in zip(keeps, received)]
    return (jnp.concatenate(outs, axis=1), norms)


def solution(mesh):
    return jax.shard_map(
        on_device,
        mesh=mesh,
        in_specs=(P("dp", "seq", None), P("dp", "seq", None)),
        out_specs=(P("dp", "seq"), P("dp")),
        check_vma=False,
    )
```

```python
import functools
import math

import jax
import jax.numpy as jnp
from jax import lax
from jax.experimental import pallas as pl
from jax.experimental.pallas import tpu as pltpu
from jax.sharding import PartitionSpec as P

ORDERS = ((4, 12, 1, 3), (12, 4, 3, 1), (1, 3, 4, 12), (3, 1, 12, 4))
WIDTHS = (640, 640, 512, 512)


def block_order(masks):
    order = [0]
    for mask in reversed(masks):
        order = order + [mask ^ k for k in order]
    return order


def exchange(value, axis, mask):
    return lax.ppermute(value, axis, [(i, i ^ mask) for i in range(lax.axis_size(axis))])


def products_kernel(
    order_ref, place_ref, scale_ref, *refs, groups, first, count, widths, examples, own, partner, base
):
    n = len(groups)
    refs = list(refs)

    def take(k):
        taken = refs[:k]
        del refs[:k]
        return taken

    if own:
        (a_ref,) = take(1)
        g_refs = take(n)
    if partner:
        own_refs, other_refs, partner_refs = take(n), take(n), take(n)
    if base:
        base_refs = take(n)
    out_refs = take(n)
    lhs, rhs, out_buf, in_sems, out_sems = refs
    depth = lhs.shape[2]
    rows = lhs.shape[1]
    block = rows // count
    tokens = depth // (own + partner)
    lanes = tokens // place_ref.shape[0]
    blocks = order_ref.shape[0] // len(widths)
    slab = lanes // examples

    def loads(i):
        v, slot = groups[i], i % 2
        w = widths[v]
        low = widths[v - 1] if v % 2 else 0
        pairs = []
        start = 0
        if own:
            pairs.append((g_refs[i].at[:, pl.ds(low, w)], rhs.at[slot, pl.ds(0, tokens), pl.ds(0, w)]))
            for j in range(count):
                pairs.append(
                    (
                        a_ref.at[order_ref[v * blocks + first + j]],
                        lhs.at[slot, pl.ds(j * block, block), pl.ds(0, tokens)],
                    )
                )
            start = tokens
        if partner:
            for k, ref in enumerate((own_refs[i], other_refs[i])):
                size = ref.shape[1]
                pairs.append(
                    (ref.at[pl.ds(first * block, rows)], lhs.at[slot, :, pl.ds(start + k * size, size)])
                )
            for k in range(place_ref.shape[0]):
                source = pl.multiple_of(place_ref[k] * lanes, lanes)
                pairs.append(
                    (
                        partner_refs[i].at[pl.ds(source, lanes)],
                        rhs.at[slot, pl.ds(start + k * lanes, lanes), pl.ds(0, w)],
                    )
                )
        if base:
            pairs.append((base_refs[i], out_buf.at[slot, :, pl.ds(0, w)]))
        return [pltpu.make_async_copy(src, dst, in_sems.at[slot, k]) for k, (src, dst) in enumerate(pairs)]

    def store(i):
        slot = i % 2
        return pltpu.make_async_copy(out_buf.at[slot, :, pl.ds(0, widths[groups[i]])], out_refs[i], out_sems.at[slot])

    for copy in loads(0):
        copy.start()
    for i in range(n):
        v, slot = groups[i], i % 2
        w = widths[v]
        if i + 1 < n:
            if i >= 1:
                store(i - 1).wait()
            for copy in loads(i + 1):
                copy.start()
        for copy in loads(i):
            copy.wait()
        for r in range(depth // slab):
            whose = order_ref[v * blocks + (0 if own and r < tokens // slab else blocks // 2)]
            part = pl.ds(r * slab, slab)
            value = rhs[slot, part, :w].astype(jnp.float32) * scale_ref[whose * examples + r % examples]
            rhs[slot, part, :w] = value.astype(rhs.dtype)
        step = rows // 2
        for m in range(2):
            part = pl.ds(m * step, step)
            total = jnp.dot(lhs[slot, part], rhs[slot, :, :w], preferred_element_type=jnp.float32)
            if base:
                total += out_buf[slot, part, :w].astype(jnp.float32)
            out_buf[slot, part, :w] = total.astype(out_buf.dtype)
        store(i).start()
    for i in range(max(n - 2, 0), n):
        store(i).wait()


def products(
    groups, order, place, scale, examples, first, count, own=None, partner=None, base=None, hint=1
):
    n = len(groups)
    operands, pieces = [], 0
    if own is not None:
        a_blocks, g = own
        operands += [a_blocks, *[g[v // 2] for v in groups]]
        blocks, block, tokens = a_blocks.shape
        pieces += 1 + count
    if partner is not None:
        for values in partner:
            operands += [values[v] for v in groups]
        tokens = partner[2][0].shape[0]
        block = partner[0][0].shape[0] // (2 * count)
        pieces += 2 + place.shape[0]
    if base is not None:
        operands += [base[v] for v in groups]
        pieces += 1
    rows = count * block
    depth = tokens * ((own is not None) + (partner is not None))
    widths = tuple(WIDTHS[v] for v in groups)
    widest = max(widths)
    anywhere = pl.BlockSpec(memory_space=pl.ANY)
    smem = pl.BlockSpec(memory_space=pltpu.SMEM)
    return pl.pallas_call(
        functools.partial(
            products_kernel,
            groups=groups,
            first=first,
            count=count,
            widths=WIDTHS,
            examples=examples,
            own=own is not None,
            partner=partner is not None,
            base=base is not None,
        ),
        in_specs=[smem, smem, smem] + [anywhere] * len(operands),
        out_specs=[anywhere] * n,
        out_shape=[jax.ShapeDtypeStruct((rows, w), jnp.bfloat16) for w in widths],
        scratch_shapes=[
            pltpu.VMEM((2, rows, depth), jnp.bfloat16),
            pltpu.VMEM((2, depth, widest), jnp.bfloat16),
            pltpu.VMEM((2, rows, widest), jnp.bfloat16),
            pltpu.SemaphoreType.DMA((2, pieces)),
            pltpu.SemaphoreType.DMA((2,)),
        ],
        compiler_params=pltpu.CompilerParams(vmem_limit_bytes=58 * 1024 * 1024),
        cost_estimate=pl.CostEstimate(
            flops=int(hint * 2 * rows * depth * sum(widths)),
            bytes_accessed=int(hint * 2 * (n * rows * depth + (depth + rows) * sum(widths))),
            transcendentals=0,
        ),
    )(order, place, scale, *operands)


def pick_near_kernel(index_ref, *refs, sources):
    step, steps = pl.program_id(0), pl.num_programs(0)
    in_refs, out_refs = refs[:sources], refs[sources:]
    half, _, lanes = in_refs[0].shape
    for v, out_ref in enumerate(out_refs):
        b = index_ref[v * steps + step]

        def put(refs, row):
            for k, in_ref in enumerate(refs):
                out_ref[:, k * lanes : (k + 1) * lanes] = in_ref[row]

        @pl.when(b < half)
        def _():
            put(in_refs[::2], jnp.minimum(b, half - 1))

        @pl.when(b >= half)
        def _():
            put(in_refs[1::2], jnp.maximum(b - half, 0))


def pick_near(pieces, index, n, block):
    lanes = pieces[0].shape[1]
    count = index.shape[0] // n
    pieces = [piece.reshape(-1, block, lanes) for piece in pieces]
    total = (len(pieces) // 2 + 1) * lanes
    return pl.pallas_call(
        functools.partial(pick_near_kernel, sources=len(pieces)),
        grid_spec=pltpu.PrefetchScalarGridSpec(
            num_scalar_prefetch=1,
            grid=(count,),
            in_specs=[pl.BlockSpec(piece.shape, lambda i, ref: (0, 0, 0)) for piece in pieces],
            out_specs=[pl.BlockSpec((block, total), lambda i, ref: (i, 0)) for _ in range(n)],
        ),
        out_shape=[jax.ShapeDtypeStruct((count * block, total), jnp.bfloat16) for _ in range(n)],
        compiler_params=pltpu.CompilerParams(vmem_limit_bytes=40 * 1024 * 1024),
        cost_estimate=pl.CostEstimate(flops=0, bytes_accessed=n * count * block, transcendentals=0),
    )(index, *pieces)


def pick_far_kernel(index_ref, top_ref, bottom_ref, *refs):
    step, steps = pl.program_id(0), pl.num_programs(0)
    half = top_ref.shape[0]
    out_refs = refs[len(refs) // 2 :]
    for v, out_ref in enumerate(out_refs):
        b = index_ref[v * steps + step]

        @pl.when(b < half)
        def _():
            out_ref[...] = top_ref[jnp.minimum(b, half - 1)]

        @pl.when(b >= half)
        def _():
            out_ref[...] = bottom_ref[jnp.maximum(b - half, 0)]


def pick_far(top, bottom, index, near, block):
    lanes = top.shape[1]
    n = len(near)
    count = index.shape[0] // n
    last = near[0].shape[1] // lanes - 1
    halves = [piece.reshape(-1, block, lanes) for piece in (top, bottom)]
    return pl.pallas_call(
        pick_far_kernel,
        grid_spec=pltpu.PrefetchScalarGridSpec(
            num_scalar_prefetch=1,
            grid=(count,),
            in_specs=[pl.BlockSpec(piece.shape, lambda i, ref: (0, 0, 0)) for piece in halves]
            + [pl.BlockSpec(memory_space=pl.ANY)] * n,
            out_specs=[pl.BlockSpec((block, lanes), lambda i, ref: (i, last)) for _ in range(n)],
        ),
        out_shape=[jax.ShapeDtypeStruct(value.shape, value.dtype) for value in near],
        input_output_aliases={3 + v: v for v in range(n)},
        compiler_params=pltpu.CompilerParams(vmem_limit_bytes=40 * 1024 * 1024),
        cost_estimate=pl.CostEstimate(flops=0, bytes_accessed=4 * n * count * block * lanes, transcendentals=0),
    )(index, *halves, *near)


def turn_kernel(in_ref, top_ref, bottom_ref):
    first_half = pl.program_id(0) < pl.num_programs(0) // 2

    @pl.when(first_half)
    def _():
        top_ref[...] = in_ref[...].T

    @pl.when(jnp.logical_not(first_half))
    def _():
        bottom_ref[...] = in_ref[...].T


def turn(value):
    tokens, width = value.shape
    steps = 4
    block = (width // steps, tokens)
    return pl.pallas_call(
        turn_kernel,
        grid=(steps,),
        in_specs=[pl.BlockSpec((tokens, width // steps), lambda i: (0, i))],
        out_specs=[
            pl.BlockSpec(block, lambda i: (jnp.minimum(i, steps // 2 - 1), 0)),
            pl.BlockSpec(block, lambda i: (jnp.maximum(i - steps // 2, 0), 0)),
        ],
        out_shape=[jax.ShapeDtypeStruct((width // 2, tokens), value.dtype)] * 2,
    )(value)


def join_kernel(place_ref, *refs):
    *in_refs, out_ref = refs
    lanes = in_refs[0].shape[1]
    first_half = pl.program_id(0) < pl.num_programs(0) // 2

    def put(half):
        for k in range(len(in_refs) // 2):
            start = pl.multiple_of(place_ref[k] * lanes, lanes)
            out_ref[:, pl.ds(start, lanes)] = in_refs[2 * k + half][...]

    @pl.when(first_half)
    def _():
        put(0)

    @pl.when(jnp.logical_not(first_half))
    def _():
        put(1)


def join(place, pieces):
    rows, lanes = pieces[0].shape
    steps = 8
    block = 2 * rows // steps
    top = pl.BlockSpec((block, lanes), lambda i, ref: (jnp.minimum(i, steps // 2 - 1), 0))
    bottom = pl.BlockSpec((block, lanes), lambda i, ref: (jnp.maximum(i - steps // 2, 0), 0))
    count = len(pieces) // 2
    return pl.pallas_call(
        join_kernel,
        grid_spec=pltpu.PrefetchScalarGridSpec(
            num_scalar_prefetch=1,
            grid=(steps,),
            in_specs=[top, bottom] * count,
            out_specs=pl.BlockSpec((block, count * lanes), lambda i, ref: (i, 0)),
        ),
        out_shape=jax.ShapeDtypeStruct((2 * rows, count * lanes), pieces[0].dtype),
        cost_estimate=pl.CostEstimate(flops=0, bytes_accessed=8 * count * rows * lanes, transcendentals=0),
    )(place, *pieces)


def split_kernel(in_ref, *out_refs):
    low = 0
    for out_ref in out_refs:
        size = out_ref.shape[2]
        out_ref[0] = in_ref[:, low : low + size]
        low += size


def split(value, n, widths):
    rows, total = value.shape
    return pl.pallas_call(
        split_kernel,
        grid=(n,),
        in_specs=[pl.BlockSpec((rows, total // n), lambda i: (0, i))],
        out_specs=[pl.BlockSpec((1, rows, w), lambda i: (i, 0, 0)) for w in widths],
        out_shape=[jax.ShapeDtypeStruct((n, rows, w), value.dtype) for w in widths],
        cost_estimate=pl.CostEstimate(flops=0, bytes_accessed=rows * total // 16, transcendentals=0),
    )(value)


def add(a, b):
    return (a.astype(jnp.float32) + b.astype(jnp.float32)).astype(jnp.bfloat16)


def on_device(acts, grads):
    seq_count = lax.axis_size("seq")
    replica_count = lax.axis_size("dp")
    examples, local_len, width = acts.shape
    hidden = grads.shape[2]
    local = examples * local_len
    tokens = seq_count * local
    block = width // replica_count
    me = lax.axis_index("dp")

    me_seq = lax.axis_index("seq")
    x, core = me_seq // 2, me_seq % 2
    place = [2 * ((x + shift) % (seq_count // 2)) + c for c in (core, 1 - core) for shift in (0, 3, 1, 2)]
    half = replica_count // 2
    order = me ^ jnp.array([block_order(masks) for masks in ORDERS], jnp.int32)
    tables = (jnp.stack(place).astype(jnp.int32), order.reshape(-1), order[:, half:].reshape(-1))
    up = [(i, (i + 2) % seq_count) for i in range(seq_count)]
    down = [(i, (i - 2) % seq_count) for i in range(seq_count)]
    groups = len(ORDERS)

    top, bottom = turn(acts.reshape(local, width))
    below_top, above_bottom = lax.ppermute(top, "seq", up), lax.ppermute(bottom, "seq", down)
    below_bottom, above_top = lax.ppermute(bottom, "seq", up), lax.ppermute(top, "seq", down)
    below_top, above_bottom, (place, order, sent_order) = lax.optimization_barrier(
        (below_top, above_bottom, tables)
    )
    far_top = lax.ppermute(below_top, "seq", up)
    far_bottom = lax.ppermute(above_bottom, "seq", down)
    below_bottom, above_top, pieces = lax.optimization_barrier(
        (below_bottom, above_top, split(grads.reshape(local, hidden), seq_count, (sum(WIDTHS[:2]), sum(WIDTHS[2:]))))
    )
    near_pieces = [top, bottom, below_top, below_bottom, above_top, above_bottom]
    near = pick_near(near_pieces, sent_order, groups, block)
    pieces, far_top, far_bottom, near = lax.optimization_barrier((pieces, far_top, far_bottom, near))
    g = [lax.all_to_all(piece, "seq", split_axis=0, concat_axis=0, tiled=True) for piece in pieces]
    g = [value.reshape(tokens, -1) for value in g]

    sent_rows = pick_far(far_top, far_bottom, sent_order, near, block)
    own_rows = [exchange(value, "dp", masks[0]) for value, masks in zip(sent_rows, ORDERS)]

    own = near_pieces + [far_top, far_bottom]
    a_t = join(place, own + [exchange(piece, "seq", 1) for piece in own])
    a_blocks = a_t.reshape(replica_count, block, tokens)
    example = (jnp.arange(tokens) // local_len) % examples
    same = example[:, None] == example[None, :]
    act_gram = lax.dot_general(a_t, a_t, (((0,), (0,)), ((), ())), preferred_element_type=jnp.float32)
    act_gram = jnp.where(same, act_gram, 0.0)

    def pairing(value):
        gram = lax.dot_general(value, value, (((1,), (1,)), ((), ())), preferred_element_type=jnp.float32)
        return jnp.sum(act_gram * gram, axis=1)

    def columns_of(v, value):
        low = WIDTHS[v - 1] if v % 2 else 0
        return value[:, low : low + WIDTHS[v]]

    parts = [columns_of(v, g[0]) for v in (0, 1)]
    rows_sum, parts, g = lax.optimization_barrier((pairing(g[0]), parts, g))
    parts += [columns_of(v, g[1]) for v in (2, 3)]
    rows_sum = rows_sum + pairing(g[1])
    rows_sum, parts, g, own_rows = lax.optimization_barrier((rows_sum, parts, g, own_rows))
    partner = [exchange(piece, "dp", masks[0]) for piece, masks in zip(parts, ORDERS)]
    other_rows = [exchange(value, "seq", 1) for value in own_rows[:2]]
    rows_sum, other_rows = lax.optimization_barrier((rows_sum, other_rows))
    partial_value = jnp.sum(rows_sum.reshape(seq_count, examples, local_len), axis=(0, 2))
    for mask in (1, 2, 6):
        partial_value = partial_value + exchange(partial_value, "seq", mask)
    norms = jnp.sqrt(partial_value)
    factor = math.sqrt(width * hidden / (examples * replica_count))

    def scale_of(norm):
        return jnp.minimum(1.0, 1.0 / (norm + 1e-06)) * factor

    quarter = half // 2
    make = functools.partial(products, order=order, place=place, examples=examples, count=quarter)
    known = jnp.broadcast_to(jnp.pad(norms, (0, 128 - examples))[None, None], (replica_count, 8, 128))
    known = lax.all_to_all(known, "dp", split_axis=0, concat_axis=0, tiled=True)
    scale = jnp.tile(scale_of(norms), replica_count)
    base = make((0, 1), scale=scale, first=quarter, own=(a_blocks, g), hint=0.02)
    known, base, partner, other_rows, own_rows = lax.optimization_barrier(
        (known, base, partner, other_rows, own_rows)
    )
    other_rows += [exchange(value, "seq", 1) for value in own_rows[2:]]
    scale = scale_of(known[:, 0, :examples].reshape(-1))
    sends = make((0, 1), scale=scale, first=quarter, partner=(own_rows, other_rows, partner), base=base)
    sends, other_rows = lax.optimization_barrier((sends, other_rows))
    theirs = (own_rows, other_rows, partner)
    sends = [*sends, *make((2, 3), scale=scale, first=quarter, own=(a_blocks, g), partner=theirs)]
    keeps = make((0, 1, 2, 3), scale=scale, first=0, own=(a_blocks, g), partner=theirs, hint=0.02)

    received = [exchange(send, "dp", masks[1]) for send, masks in zip(sends, ORDERS)]
    for step in (2, 3):
        rows = keeps[0].shape[0] // 2
        sends = [add(keeps[v][rows:], received[v][rows:]) for v in (0, 1)]
        sends, received[2:] = lax.optimization_barrier((sends, received[2:]))
        sends += [add(keeps[v][rows:], received[v][rows:]) for v in (2, 3)]
        sends = lax.optimization_barrier(sends)
        sent = [exchange(send, "dp", masks[step]) for send, masks in zip(sends, ORDERS)]
        keeps = [add(keep[:rows], value[:rows]) for keep, value in zip(keeps, received)]
        received = sent
    outs = [add(keep, value) for keep, value in zip(keeps, received)]
    return (jnp.concatenate(outs, axis=1), norms)


def solution(mesh):
    return jax.shard_map(
        on_device,
        mesh=mesh,
        in_specs=(P("dp", "seq", None), P("dp", "seq", None)),
        out_specs=(P("dp", "seq"), P("dp")),
        check_vma=False,
    )
```

```python
import functools
import math

import jax
import jax.numpy as jnp
from jax import lax
from jax.experimental import pallas as pl
from jax.experimental.pallas import tpu as pltpu
from jax.sharding import PartitionSpec as P

ORDERS = ((4, 12, 1, 3), (12, 4, 3, 1), (1, 3, 4, 12), (3, 1, 12, 4))
WIDTHS = (640, 640, 512, 512)


def block_order(masks):
    order = [0]
    for mask in reversed(masks):
        order = order + [mask ^ k for k in order]
    return order


def exchange(value, axis, mask):
    return lax.ppermute(value, axis, [(i, i ^ mask) for i in range(lax.axis_size(axis))])


def products_kernel(
    order_ref, place_ref, scale_ref, *refs, groups, first, count, widths, examples, own, partner, base
):
    n = len(groups)
    refs = list(refs)

    def take(k):
        taken = refs[:k]
        del refs[:k]
        return taken

    if own:
        (a_ref,) = take(1)
        g_refs = take(n)
    if partner:
        own_refs, other_refs, partner_refs = take(n), take(n), take(n)
    if base:
        base_refs = take(n)
    out_refs = take(n)
    lhs, rhs, out_buf, in_sems, out_sems = refs
    depth = lhs.shape[2]
    rows = lhs.shape[1]
    block = rows // count
    tokens = depth // (own + partner)
    lanes = tokens // place_ref.shape[0]
    blocks = order_ref.shape[0] // len(widths)
    slab = lanes // examples

    def loads(i):
        v, slot = groups[i], i % 2
        w = widths[v]
        low = widths[v - 1] if v % 2 else 0
        pairs = []
        start = 0
        if own:
            pairs.append((g_refs[i].at[:, pl.ds(low, w)], rhs.at[slot, pl.ds(0, tokens), pl.ds(0, w)]))
            for j in range(count):
                pairs.append(
                    (
                        a_ref.at[order_ref[v * blocks + first + j]],
                        lhs.at[slot, pl.ds(j * block, block), pl.ds(0, tokens)],
                    )
                )
            start = tokens
        if partner:
            for k, ref in enumerate((own_refs[i], other_refs[i])):
                size = ref.shape[1]
                pairs.append(
                    (ref.at[pl.ds(first * block, rows)], lhs.at[slot, :, pl.ds(start + k * size, size)])
                )
            for k in range(place_ref.shape[0]):
                source = pl.multiple_of(place_ref[k] * lanes, lanes)
                pairs.append(
                    (
                        partner_refs[i].at[pl.ds(source, lanes)],
                        rhs.at[slot, pl.ds(start + k * lanes, lanes), pl.ds(0, w)],
                    )
                )
        if base:
            pairs.append((base_refs[i], out_buf.at[slot, :, pl.ds(0, w)]))
        return [pltpu.make_async_copy(src, dst, in_sems.at[slot, k]) for k, (src, dst) in enumerate(pairs)]

    def store(i):
        slot = i % 2
        return pltpu.make_async_copy(out_buf.at[slot, :, pl.ds(0, widths[groups[i]])], out_refs[i], out_sems.at[slot])

    for copy in loads(0):
        copy.start()
    for i in range(n):
        v, slot = groups[i], i % 2
        w = widths[v]
        if i + 1 < n:
            if i >= 1:
                store(i - 1).wait()
            for copy in loads(i + 1):
                copy.start()
        for copy in loads(i):
            copy.wait()
        for r in range(depth // slab):
            whose = order_ref[v * blocks + (0 if own and r < tokens // slab else blocks // 2)]
            part = pl.ds(r * slab, slab)
            value = rhs[slot, part, :w].astype(jnp.float32) * scale_ref[whose * examples + r % examples]
            rhs[slot, part, :w] = value.astype(rhs.dtype)
        step = rows // 2
        for m in range(2):
            part = pl.ds(m * step, step)
            total = jnp.dot(lhs[slot, part], rhs[slot, :, :w], preferred_element_type=jnp.float32)
            if base:
                total += out_buf[slot, part, :w].astype(jnp.float32)
            out_buf[slot, part, :w] = total.astype(out_buf.dtype)
        store(i).start()
    for i in range(max(n - 2, 0), n):
        store(i).wait()


def products(
    groups, order, place, scale, examples, first, count, own=None, partner=None, base=None, hint=1
):
    n = len(groups)
    operands, pieces = [], 0
    if own is not None:
        a_blocks, g = own
        operands += [a_blocks, *[g[v // 2] for v in groups]]
        blocks, block, tokens = a_blocks.shape
        pieces += 1 + count
    if partner is not None:
        for values in partner:
            operands += [values[v] for v in groups]
        tokens = partner[2][0].shape[0]
        block = partner[0][0].shape[0] // (2 * count)
        pieces += 2 + place.shape[0]
    if base is not None:
        operands += [base[v] for v in groups]
        pieces += 1
    rows = count * block
    depth = tokens * ((own is not None) + (partner is not None))
    widths = tuple(WIDTHS[v] for v in groups)
    widest = max(widths)
    anywhere = pl.BlockSpec(memory_space=pl.ANY)
    smem = pl.BlockSpec(memory_space=pltpu.SMEM)
    return pl.pallas_call(
        functools.partial(
            products_kernel,
            groups=groups,
            first=first,
            count=count,
            widths=WIDTHS,
            examples=examples,
            own=own is not None,
            partner=partner is not None,
            base=base is not None,
        ),
        in_specs=[smem, smem, smem] + [anywhere] * len(operands),
        out_specs=[anywhere] * n,
        out_shape=[jax.ShapeDtypeStruct((rows, w), jnp.bfloat16) for w in widths],
        scratch_shapes=[
            pltpu.VMEM((2, rows, depth), jnp.bfloat16),
            pltpu.VMEM((2, depth, widest), jnp.bfloat16),
            pltpu.VMEM((2, rows, widest), jnp.bfloat16),
            pltpu.SemaphoreType.DMA((2, pieces)),
            pltpu.SemaphoreType.DMA((2,)),
        ],
        compiler_params=pltpu.CompilerParams(vmem_limit_bytes=58 * 1024 * 1024),
        cost_estimate=pl.CostEstimate(
            flops=int(hint * 2 * rows * depth * sum(widths)),
            bytes_accessed=int(hint * 2 * (n * rows * depth + (depth + rows) * sum(widths))),
            transcendentals=0,
        ),
    )(order, place, scale, *operands)


def pick_near_kernel(index_ref, *refs, sources):
    step, steps = pl.program_id(0), pl.num_programs(0)
    in_refs, out_refs = refs[:sources], refs[sources:]
    half, _, lanes = in_refs[0].shape
    for v, out_ref in enumerate(out_refs):
        b = index_ref[v * steps + step]

        def put(refs, row):
            for k, in_ref in enumerate(refs):
                out_ref[:, k * lanes : (k + 1) * lanes] = in_ref[row]

        @pl.when(b < half)
        def _():
            put(in_refs[::2], jnp.minimum(b, half - 1))

        @pl.when(b >= half)
        def _():
            put(in_refs[1::2], jnp.maximum(b - half, 0))


def pick_near(pieces, index, n, block):
    lanes = pieces[0].shape[1]
    count = index.shape[0] // n
    pieces = [piece.reshape(-1, block, lanes) for piece in pieces]
    total = (len(pieces) // 2 + 1) * lanes
    return pl.pallas_call(
        functools.partial(pick_near_kernel, sources=len(pieces)),
        grid_spec=pltpu.PrefetchScalarGridSpec(
            num_scalar_prefetch=1,
            grid=(count,),
            in_specs=[pl.BlockSpec(piece.shape, lambda i, ref: (0, 0, 0)) for piece in pieces],
            out_specs=[pl.BlockSpec((block, total), lambda i, ref: (i, 0)) for _ in range(n)],
        ),
        out_shape=[jax.ShapeDtypeStruct((count * block, total), jnp.bfloat16) for _ in range(n)],
        compiler_params=pltpu.CompilerParams(vmem_limit_bytes=40 * 1024 * 1024),
        cost_estimate=pl.CostEstimate(flops=0, bytes_accessed=n * count * block, transcendentals=0),
    )(index, *pieces)


def pick_far_kernel(index_ref, top_ref, bottom_ref, *refs):
    step, steps = pl.program_id(0), pl.num_programs(0)
    half = top_ref.shape[0]
    out_refs = refs[len(refs) // 2 :]
    for v, out_ref in enumerate(out_refs):
        b = index_ref[v * steps + step]

        @pl.when(b < half)
        def _():
            out_ref[...] = top_ref[jnp.minimum(b, half - 1)]

        @pl.when(b >= half)
        def _():
            out_ref[...] = bottom_ref[jnp.maximum(b - half, 0)]


def pick_far(top, bottom, index, near, block):
    lanes = top.shape[1]
    n = len(near)
    count = index.shape[0] // n
    last = near[0].shape[1] // lanes - 1
    halves = [piece.reshape(-1, block, lanes) for piece in (top, bottom)]
    return pl.pallas_call(
        pick_far_kernel,
        grid_spec=pltpu.PrefetchScalarGridSpec(
            num_scalar_prefetch=1,
            grid=(count,),
            in_specs=[pl.BlockSpec(piece.shape, lambda i, ref: (0, 0, 0)) for piece in halves]
            + [pl.BlockSpec(memory_space=pl.ANY)] * n,
            out_specs=[pl.BlockSpec((block, lanes), lambda i, ref: (i, last)) for _ in range(n)],
        ),
        out_shape=[jax.ShapeDtypeStruct(value.shape, value.dtype) for value in near],
        input_output_aliases={3 + v: v for v in range(n)},
        compiler_params=pltpu.CompilerParams(vmem_limit_bytes=40 * 1024 * 1024),
        cost_estimate=pl.CostEstimate(flops=0, bytes_accessed=4 * n * count * block * lanes, transcendentals=0),
    )(index, *halves, *near)


def turn_kernel(in_ref, top_ref, bottom_ref):
    first_half = pl.program_id(0) < pl.num_programs(0) // 2

    @pl.when(first_half)
    def _():
        top_ref[...] = in_ref[...].T

    @pl.when(jnp.logical_not(first_half))
    def _():
        bottom_ref[...] = in_ref[...].T


def turn(value):
    tokens, width = value.shape
    steps = 4
    block = (width // steps, tokens)
    return pl.pallas_call(
        turn_kernel,
        grid=(steps,),
        in_specs=[pl.BlockSpec((tokens, width // steps), lambda i: (0, i))],
        out_specs=[
            pl.BlockSpec(block, lambda i: (jnp.minimum(i, steps // 2 - 1), 0)),
            pl.BlockSpec(block, lambda i: (jnp.maximum(i - steps // 2, 0), 0)),
        ],
        out_shape=[jax.ShapeDtypeStruct((width // 2, tokens), value.dtype)] * 2,
    )(value)


def join_kernel(place_ref, *refs):
    *in_refs, out_ref = refs
    lanes = in_refs[0].shape[1]
    first_half = pl.program_id(0) < pl.num_programs(0) // 2

    def put(half):
        for k in range(len(in_refs) // 2):
            start = pl.multiple_of(place_ref[k] * lanes, lanes)
            out_ref[:, pl.ds(start, lanes)] = in_refs[2 * k + half][...]

    @pl.when(first_half)
    def _():
        put(0)

    @pl.when(jnp.logical_not(first_half))
    def _():
        put(1)


def join(place, pieces):
    rows, lanes = pieces[0].shape
    steps = 8
    block = 2 * rows // steps
    top = pl.BlockSpec((block, lanes), lambda i, ref: (jnp.minimum(i, steps // 2 - 1), 0))
    bottom = pl.BlockSpec((block, lanes), lambda i, ref: (jnp.maximum(i - steps // 2, 0), 0))
    count = len(pieces) // 2
    return pl.pallas_call(
        join_kernel,
        grid_spec=pltpu.PrefetchScalarGridSpec(
            num_scalar_prefetch=1,
            grid=(steps,),
            in_specs=[top, bottom] * count,
            out_specs=pl.BlockSpec((block, count * lanes), lambda i, ref: (i, 0)),
        ),
        out_shape=jax.ShapeDtypeStruct((2 * rows, count * lanes), pieces[0].dtype),
        cost_estimate=pl.CostEstimate(flops=0, bytes_accessed=8 * count * rows * lanes, transcendentals=0),
    )(place, *pieces)


def split_kernel(in_ref, *out_refs):
    low = 0
    for out_ref in out_refs:
        size = out_ref.shape[2]
        out_ref[0] = in_ref[:, low : low + size]
        low += size


def split(value, n, widths):
    rows, total = value.shape
    return pl.pallas_call(
        split_kernel,
        grid=(n,),
        in_specs=[pl.BlockSpec((rows, total // n), lambda i: (0, i))],
        out_specs=[pl.BlockSpec((1, rows, w), lambda i: (i, 0, 0)) for w in widths],
        out_shape=[jax.ShapeDtypeStruct((n, rows, w), value.dtype) for w in widths],
        cost_estimate=pl.CostEstimate(flops=0, bytes_accessed=rows * total // 16, transcendentals=0),
    )(value)


def add(a, b):
    return (a.astype(jnp.float32) + b.astype(jnp.float32)).astype(jnp.bfloat16)


def on_device(acts, grads):
    seq_count = lax.axis_size("seq")
    replica_count = lax.axis_size("dp")
    examples, local_len, width = acts.shape
    hidden = grads.shape[2]
    local = examples * local_len
    tokens = seq_count * local
    block = width // replica_count
    me = lax.axis_index("dp")

    me_seq = lax.axis_index("seq")
    x, core = me_seq // 2, me_seq % 2
    place = [2 * ((x + shift) % (seq_count // 2)) + c for c in (core, 1 - core) for shift in (0, 3, 1, 2)]
    half = replica_count // 2
    order = me ^ jnp.array([block_order(masks) for masks in ORDERS], jnp.int32)
    tables = (jnp.stack(place).astype(jnp.int32), order.reshape(-1), order[:, half:].reshape(-1))
    up = [(i, (i + 2) % seq_count) for i in range(seq_count)]
    down = [(i, (i - 2) % seq_count) for i in range(seq_count)]
    groups = len(ORDERS)

    top, bottom = turn(acts.reshape(local, width))
    below_top, above_bottom = lax.ppermute(top, "seq", up), lax.ppermute(bottom, "seq", down)
    below_bottom, above_top = lax.ppermute(bottom, "seq", up), lax.ppermute(top, "seq", down)
    below_top, above_bottom, (place, order, sent_order) = lax.optimization_barrier(
        (below_top, above_bottom, tables)
    )
    far_top = lax.ppermute(below_top, "seq", up)
    far_bottom = lax.ppermute(above_bottom, "seq", down)
    below_bottom, above_top, pieces = lax.optimization_barrier(
        (below_bottom, above_top, split(grads.reshape(local, hidden), seq_count, (sum(WIDTHS[:2]), sum(WIDTHS[2:]))))
    )
    near_pieces = [top, bottom, below_top, below_bottom, above_top, above_bottom]
    near = pick_near(near_pieces, sent_order, groups, block)
    pieces, far_top, far_bottom, near = lax.optimization_barrier((pieces, far_top, far_bottom, near))
    g = [lax.all_to_all(piece, "seq", split_axis=0, concat_axis=0, tiled=True) for piece in pieces]
    g = [value.reshape(tokens, -1) for value in g]

    sent_rows = pick_far(far_top, far_bottom, sent_order, near, block)
    own_rows = [exchange(value, "dp", masks[0]) for value, masks in zip(sent_rows, ORDERS)]

    own, sent_rows = lax.optimization_barrier((near_pieces + [far_top, far_bottom], sent_rows))
    a_t = join(place, own + [exchange(piece, "seq", 1) for piece in own])
    a_blocks = a_t.reshape(replica_count, block, tokens)
    side = tokens // 2
    example = (jnp.arange(side) // local_len) % examples
    same = example[:, None] == example[None, :]

    def blocks_of(first, second, dim):
        pairs = ((first, first, 1.0), (first, second, 2.0), (second, second, 1.0))
        return [
            (weight if dim else 1.0) * lax.dot_general(p, q, (((dim,), (dim,)), ((), ())), preferred_element_type=jnp.float32)
            for p, q, weight in pairs
        ]

    a_now, g[0] = lax.optimization_barrier((a_t, g[0]))
    act_gram = [jnp.where(same, gram, 0.0) for gram in blocks_of(a_now[:, :side], a_now[:, side:], 0)]

    def pairing(value):
        grams = blocks_of(value[:side], value[side:], 1)
        return sum(jnp.sum(a * g, axis=1) for a, g in zip(act_gram, grams))

    def columns_of(v, value):
        low = WIDTHS[v - 1] if v % 2 else 0
        return value[:, low : low + WIDTHS[v]]

    parts = [columns_of(v, g[0]) for v in (0, 1)]
    rows_sum, parts, g = lax.optimization_barrier((pairing(g[0]), parts, g))
    parts += [columns_of(v, g[1]) for v in (2, 3)]
    rows_sum = rows_sum + pairing(g[1])
    rows_sum, parts, g, own_rows = lax.optimization_barrier((rows_sum, parts, g, own_rows))
    partner = [exchange(piece, "dp", masks[0]) for piece, masks in zip(parts, ORDERS)]
    other_rows = [exchange(value, "seq", 1) for value in own_rows[:2]]
    rows_sum, other_rows = lax.optimization_barrier((rows_sum, other_rows))
    partial_value = jnp.sum(rows_sum.reshape(seq_count // 2, examples, local_len), axis=(0, 2))
    for mask in (1, 2, 6):
        partial_value = partial_value + exchange(partial_value, "seq", mask)
    norms = jnp.sqrt(partial_value)
    factor = math.sqrt(width * hidden / (examples * replica_count))

    def scale_of(norm):
        return jnp.minimum(1.0, 1.0 / (norm + 1e-06)) * factor

    quarter = half // 2
    make = functools.partial(products, order=order, place=place, examples=examples, count=quarter)
    known = jnp.broadcast_to(jnp.pad(norms, (0, 128 - examples))[None, None], (replica_count, 8, 128))
    known = lax.all_to_all(known, "dp", split_axis=0, concat_axis=0, tiled=True)
    scale = jnp.tile(scale_of(norms), replica_count)
    base = make((0, 1), scale=scale, first=quarter, own=(a_blocks, g), hint=0.02)
    known, base, partner, other_rows, own_rows = lax.optimization_barrier(
        (known, base, partner, other_rows, own_rows)
    )
    other_rows += [exchange(value, "seq", 1) for value in own_rows[2:]]
    scale = scale_of(known[:, 0, :examples].reshape(-1))
    sends = make((0, 1), scale=scale, first=quarter, partner=(own_rows, other_rows, partner), base=base)
    sends, other_rows = lax.optimization_barrier((sends, other_rows))
    theirs = (own_rows, other_rows, partner)
    sends = [*sends, *make((2, 3), scale=scale, first=quarter, own=(a_blocks, g), partner=theirs)]
    keeps = make((0, 1, 2, 3), scale=scale, first=0, own=(a_blocks, g), partner=theirs, hint=0.02)

    received = [exchange(send, "dp", masks[1]) for send, masks in zip(sends, ORDERS)]
    for step in (2, 3):
        rows = keeps[0].shape[0] // 2
        sends = [add(keeps[v][rows:], received[v][rows:]) for v in (0, 1)]
        sends, received[2:] = lax.optimization_barrier((sends, received[2:]))
        sends += [add(keeps[v][rows:], received[v][rows:]) for v in (2, 3)]
        sends = lax.optimization_barrier(sends)
        sent = [exchange(send, "dp", masks[step]) for send, masks in zip(sends, ORDERS)]
        keeps = [add(keep[:rows], value[:rows]) for keep, value in zip(keeps, received)]
        received = sent
    outs = [add(keep, value) for keep, value in zip(keeps, received)]
    return (jnp.concatenate(outs, axis=1), norms)


def solution(mesh):
    return jax.shard_map(
        on_device,
        mesh=mesh,
        in_specs=(P("dp", "seq", None), P("dp", "seq", None)),
        out_specs=(P("dp", "seq"), P("dp")),
        check_vma=False,
    )
```
